256 devices in a mesh: band: 8 (over y, x_lo), slab: 32 (over x_hi, z, core).
Axes of the slice: x: 4 (x_hi: 2, x_lo: 2; x = x_hi * 2 + x_lo), y: 4, z: 8, core: 2. Of those that a mesh axis runs over, the one named last changes fastest.
Arguments:
- wavefunctions: float32 [8, 128, 128, 128], P('band', 'slab'), may hold values from -6 to 6
Outputs:
- exchange_field: float32 [8, 128, 128, 128], P('band', 'slab')
The draws below stay inside these ranges and needn't reach their ends.
All inputs are finite; a program needn't handle non-finite values.
Results may differ from the reference program's by a relative error of at most 0.0003.
Values sent between devices are 32-bit elements; how exact they have to be, the bound alone decides.
A program may use at most 64 MiB of HBM per device.

```python
import jax
import jax.numpy as jnp
from jax import lax

GRID = 128
BANDS = 8


def block_levels(own_key, shape, pieces, low, largest):
    level, own = 1.0, jax.random.fold_in(own_key, 6)
    for position, parts in pieces:
        draws = jnp.exp(jax.random.uniform(jax.random.fold_in(own, position), (parts,), jnp.float32, low / len(pieces), largest / len(pieces)))
        level = level * jnp.repeat(draws, shape[position] // parts).reshape([-1 if axis == position else 1 for axis in range(len(shape))])
    return level


def normal_values(stream_key, shape, width, bound, pieces=(), held_as=jnp.bfloat16):
    entries = jax.random.normal(stream_key, shape, jnp.float32) * width
    if len(pieces) > 0:
        entries = block_levels(stream_key, shape, pieces, -0.22, 0.18) * entries
    return jnp.clip(entries, min=-bound, max=bound).astype(held_as)


def setup_inputs(seed: int = 0) -> dict:
    streams_of = jax.random.split(jax.random.key(seed), 2)
    return {
        "wavefunctions": normal_values(streams_of[0], (BANDS, GRID, GRID, GRID), 1.0, 6.0, ((0, 8), (1, 32)), jnp.float32),
    }


def coulomb_kernel(length):
    folded = jnp.fft.fftfreq(length) * length
    last_freq = jnp.arange(length // 2 + 1).astype(folded.dtype)
    squared = folded[:, None, None] ** 2 + folded[None, :, None] ** 2 + last_freq[None, None, :] ** 2
    kernel_scale = length ** 1.5 / 4.0
    return jnp.where(squared > 0, kernel_scale / jnp.maximum(squared, 1.0), 0.0)


def reference(wavefunctions):
    kernel = coulomb_kernel(GRID)

    def one_band(band_field):
        density = band_field[None] * wavefunctions
        spectra = jnp.fft.rfftn(density, axes=(1, 2, 3))
        potential = jnp.fft.irfftn(spectra * kernel, s=(GRID, GRID, GRID), axes=(1, 2, 3))
        return -0.25 * jnp.sum(potential * wavefunctions, axis=0)

    return lax.map(one_band, wavefunctions)
```

```python
import functools
import math

import jax
import jax.numpy as jnp
import ml_dtypes
import numpy as np
from jax import lax
from jax.experimental import pallas as pl
from jax.experimental.pallas import tpu as pltpu
from jax.sharding import PartitionSpec as P

MESH = pl.DeviceIdType.MESH
N = 128
PEERS = 32
PLANES = 4
ROWS = PLANES * N
BF16, F32 = jnp.bfloat16, jnp.float32


def weight_tables():
    index = np.arange(N)
    angle = 2.0 * np.pi / N * (index[:, None] * index[None, :] % N)
    cos, sin = np.cos(angle), np.sin(angle)
    left = np.block([[cos, sin], [-sin, cos]])
    peer, part, sub = np.meshgrid(np.arange(PEERS), np.arange(2), np.arange(4), indexing="ij")
    y_order = (part * N + peer * 4 + sub).reshape(-1)
    part, plane, peer = np.meshgrid(np.arange(2), np.arange(PLANES), np.arange(PEERS), indexing="ij")
    x_order = (part * N + peer * PLANES + plane).reshape(-1)
    z_fwd = left.T
    y_fwd = left[y_order, :]
    x_fwd = left[:, x_order]
    stages = [z_fwd, y_fwd, x_fwd, x_fwd.T, y_fwd.T, z_fwd.T]
    tables = []
    for stage in stages:
        high = stage.astype(ml_dtypes.bfloat16)
        low = (stage - high.astype(np.float64)).astype(ml_dtypes.bfloat16)
        tables += [high, low]
    return np.stack(tables)


def halves(value):
    high = value.astype(BF16)
    return high, (value - high.astype(F32)).astype(BF16)


def mm(a, b):
    return jnp.dot(a, b, preferred_element_type=F32)


def kernel(own, wt, out, vis, kt, tmp, send_f, recv_f, send_b, recv_b, send_q, recv_q, send_qb, recv_qb,
           give, take, gather_send, gather_recv, trans_send, trans_recv, local_sem, give_send, give_recv):
    band, slab = lax.axis_index("band"), lax.axis_index("slab")
    y, xl = band // 2, band % 2
    odd = y % 2
    high = y // 2
    quarter = odd * 2 + xl
    y1, y2, y3 = y + 1 - 2 * odd, (y + 2) % 4, 3 - y
    at = lambda yy, xx: {"band": yy * 2 + xx, "slab": slab}
    xo = 1 - xl
    flip = lambda bit: xl + bit - 2 * xl * bit
    mate, near0, near1 = at(y, xo), at(y1, xl), at(y1, xo)
    c2, c2_inv = at(y3, flip(odd)), at(y3, flip(1 - odd))
    c3, c3_inv = at(y2, flip(high)), at(y2, flip(1 - high))

    def peer_of(k):
        return (slab + k) % PEERS

    barrier = pltpu.get_barrier_semaphore()

    def greet_band(k, _):
        pl.semaphore_signal(barrier, inc=1, device_id={"band": (band + k) % 8, "slab": slab}, device_id_type=MESH)
        return 0

    def greet_slab(k, _):
        pl.semaphore_signal(barrier, inc=1, device_id={"band": band, "slab": peer_of(k)}, device_id_type=MESH)
        return 0

    lax.fori_loop(1, 8, greet_band, 0)
    lax.fori_loop(1, PEERS, greet_slab, 0)
    pl.semaphore_wait(barrier, 7 + PEERS - 1)

    def gather(slot, device):
        pltpu.make_async_remote_copy(own, vis.at[slot], gather_send.at[slot], gather_recv.at[slot],
                                     device_id=device, device_id_type=MESH).start()

    def arrived(slot):
        pltpu.make_async_copy(vis.at[slot], vis.at[slot], gather_recv.at[slot]).wait()

    gather(1, near0)
    gather(2, near1)
    gather(3, c2_inv)
    gather(4, c3_inv)
    gather(0, mate)

    ky_base = slab * 4
    kx = lax.broadcasted_iota(jnp.int32, (N, N), 0)
    kz = lax.broadcasted_iota(jnp.int32, (N, N), 1)
    fold = lambda v: jnp.where(v < N // 2, v, v - N).astype(F32)
    scale = N**1.5 / 4.0 / float(N) ** 3
    plane_sq = fold(kx) ** 2 + fold(kz) ** 2
    for j in range(4):
        ky = fold(jnp.full((N, N), 0, jnp.int32) + (ky_base + j))
        squared = plane_sq + ky * ky
        kt[j] = jnp.where(squared > 0, scale / jnp.maximum(squared, 1.0), 0.0)

    def left(stage, value):
        hi, lo = halves(value)
        return mm(wt[2 * stage], hi) + mm(wt[2 * stage], lo) + mm(wt[2 * stage + 1], hi)

    def right(value, stage):
        hi, lo = halves(value)
        return mm(hi, wt[2 * stage]) + mm(lo, wt[2 * stage]) + mm(hi, wt[2 * stage + 1])

    def forward(first, second):
        spec = right(jnp.concatenate([first, second], axis=1), 0)
        parts = []
        for p in range(PLANES):
            rows = spec[p * N:(p + 1) * N]
            parts.append(jnp.concatenate([rows[:, :N], rows[:, N:]], axis=0))
        return left(1, jnp.concatenate(parts, axis=1))

    def backward(planes):
        spec = left(4, jnp.concatenate(planes, axis=1))
        rows = []
        for p in range(PLANES):
            part = spec[:, p * N:(p + 1) * N]
            rows.append(jnp.concatenate([part[:N], part[N:]], axis=1))
        both = right(jnp.concatenate(rows, axis=0), 5)
        return both[:, :N], both[:, N:]

    def convolve(columns, kern):
        spec = left(2, columns)
        return left(3, jnp.concatenate([spec[:N] * kern, spec[N:] * kern], axis=0))

    def chunk(ref, device):
        rows = pl.ds(pl.multiple_of(device * 8, 8), 8)
        return ref.at[:, rows, :] if len(ref.shape) == 3 else ref.at[rows, :]

    def exchange(source, target, sem):
        def step(k, _):
            peer = peer_of(k)
            pltpu.make_async_remote_copy(chunk(source, peer), chunk(target, slab), trans_send.at[sem], trans_recv.at[sem],
                                         device_id={"band": band, "slab": peer}, device_id_type=MESH).start()
            return 0
        lax.fori_loop(1, PEERS, step, 0)
        pltpu.make_async_copy(chunk(source, slab), chunk(target, slab), local_sem.at[sem]).start()

    def all_chunks(ref):
        return ref.at[:, pl.ds(0, 8 * (PEERS - 1)), :] if len(ref.shape) == 3 else ref.at[pl.ds(0, 8 * (PEERS - 1)), :]

    def exchanged(source, target, sem):
        pltpu.make_async_copy(chunk(source, slab), chunk(target, slab), local_sem.at[sem]).wait()
        pltpu.make_async_copy(all_chunks(target), all_chunks(target), trans_recv.at[sem]).wait()

    def sent(source, sem):
        pltpu.make_async_copy(all_chunks(source), all_chunks(source), trans_send.at[sem]).wait()

    def scatter_planes(p, value):
        for plane in range(PLANES):
            send_f[p, plane] = value[:, plane * N:(plane + 1) * N]
        exchange(send_f.at[p], recv_f.at[p], p)

    arrived(1 + odd)
    mine = own[...]
    scatter_planes(0, forward(mine * mine, mine * vis[1 + odd]))
    arrived(3)
    arrived(4)
    scatter_planes(1, forward(mine * vis[3], mine * vis[4]))
    arrived(2 - odd)
    arrived(0)
    even = odd == 0
    inner, outer = mine * vis[0], vis[1] * vis[2]
    shared = forward(jnp.where(even, inner, outer), jnp.where(even, outer, inner))
    for plane in range(PLANES):
        tmp[plane] = shared[:, plane * N:(plane + 1) * N]
    for plane in range(PLANES):
        for part in range(2):
            send_q[pl.ds(plane * 2 + part, PEERS, stride=8), :] = tmp[plane, pl.ds(part * 4 + quarter, PEERS, stride=8), :]
    exchange(send_q, recv_q, 2)

    order = [(part, plane) for part in range(2) for plane in range(PLANES)]

    for p in range(2):
        exchanged(send_f.at[p], recv_f.at[p], p)
        columns = [
            jnp.concatenate([recv_f[p, plane, pl.ds(part * 4 + j, PEERS, stride=8), :] for part, plane in order], axis=0)
            for j in range(4)
        ]
        kern = jnp.concatenate([kt[j] for j in range(4)], axis=1)
        field = convolve(jnp.concatenate(columns, axis=1), kern)
        for j in range(4):
            for i, (part, plane) in enumerate(order):
                send_b[p, plane, pl.ds(part * 4 + j, PEERS, stride=8), :] = field[i * PEERS:(i + 1) * PEERS, j * N:(j + 1) * N]
        exchange(send_b.at[p], recv_b.at[p], 3 + p)

    exchanged(send_q, recv_q, 2)
    columns = jnp.concatenate([recv_q[pl.ds(plane * 2 + part, PEERS, stride=8), :] for part, plane in order], axis=0)
    field = convolve(columns, kt[quarter])
    for i, (part, plane) in enumerate(order):
        send_qb[pl.ds(plane * 2 + part, PEERS, stride=8), :] = field[i * PEERS:(i + 1) * PEERS]
    exchange(send_qb, recv_qb, 5)

    def hand_over(slot, device):
        pltpu.make_async_remote_copy(give.at[slot], take.at[slot], give_send.at[slot], give_recv.at[slot],
                                     device_id=device, device_id_type=MESH).start()

    exchanged(send_b.at[0], recv_b.at[0], 3)
    first, second = backward([recv_b[0, plane] for plane in range(PLANES)])
    out[...] = first * own[...] + second * vis[1 + odd]
    give[1 + odd] = second * own[...]

    exchanged(send_b.at[1], recv_b.at[1], 4)
    first, second = backward([recv_b[1, plane] for plane in range(PLANES)])
    give[3] = first * own[...]
    hand_over(3, c2)
    give[4] = second * own[...]
    hand_over(4, c3)
    out[...] += first * vis[3] + second * vis[4]

    exchanged(send_qb, recv_qb, 5)
    tmp[...] = jnp.zeros(tmp.shape, F32)
    for plane in range(PLANES):
        for part in range(2):
            tmp[plane, pl.ds(part * 4 + quarter, PEERS, stride=8), :] = recv_qb[pl.ds(plane * 2 + part, PEERS, stride=8), :]
    first, second = backward([tmp[plane] for plane in range(PLANES)])
    v_in, v_out = jnp.where(even, first, second), jnp.where(even, second, first)
    give[0] = v_in * own[...]
    hand_over(0, mate)
    give[1 + odd] += v_out * vis[2 - odd]
    give[2 - odd] = v_out * vis[1 + odd]
    hand_over(1, near0)
    hand_over(2, near1)
    out[...] += v_in * vis[0]

    for slot in range(5):
        pltpu.make_async_copy(take.at[slot], take.at[slot], give_recv.at[slot]).wait()
    out[...] = -0.25 * (out[...] + take[0] + take[1] + take[2] + take[3] + take[4])

    for slot in range(5):
        pltpu.make_async_copy(own, own, gather_send.at[slot]).wait()
        pltpu.make_async_copy(give.at[slot], give.at[slot], give_send.at[slot]).wait()
    for p in range(2):
        sent(send_f.at[p], p)
        sent(send_b.at[p], 3 + p)
    sent(send_q, 2)
    sent(send_qb, 5)


def per_device(wavefunctions, tables):
    vmem = pl.BlockSpec(memory_space=pltpu.VMEM)
    dma = pltpu.SemaphoreType.DMA
    full, small = pltpu.VMEM((2, PLANES, 2 * N, N), F32), pltpu.VMEM((2 * N, N), F32)
    bands = pltpu.VMEM((5, ROWS, N), F32)
    field = pl.pallas_call(
        kernel,
        out_shape=jax.ShapeDtypeStruct((ROWS, N), F32),
        in_specs=[vmem, vmem],
        out_specs=vmem,
        scratch_shapes=[
            bands,
            pltpu.VMEM((4, N, N), F32),
            pltpu.VMEM((PLANES, 2 * N, N), F32),
            full, full, full, full,
            small, small, small, small,
            bands, bands,
            dma((5,)), dma((5,)), dma((6,)), dma((6,)), dma((6,)), dma((5,)), dma((5,)),
        ],
        compiler_params=pltpu.CompilerParams(collective_id=0, has_side_effects=True, vmem_limit_bytes=48 << 20),
        name="exchange",
    )(wavefunctions.reshape(ROWS, N), tables)
    return field.reshape(1, PLANES, N, N)


def solution(mesh):
    tables = weight_tables()
    spec = P("band", "slab", None, None)
    run = jax.shard_map(per_device, mesh=mesh, in_specs=(spec, P()), out_specs=spec, check_vma=False)
    return lambda wavefunctions: run(wavefunctions, jnp.asarray(tables))
```

```python
import jax
import jax.numpy as jnp
import ml_dtypes
import numpy as np
from jax import lax
from jax.experimental import pallas as pl
from jax.experimental.pallas import tpu as pltpu
from jax.sharding import PartitionSpec as P

MESH = pl.DeviceIdType.MESH
N = 128
CHIPS = 128
BF16, F32 = jnp.bfloat16, jnp.float32

INNER = [((0, 0), (1, 1)), ((2, 2), (3, 3)), ((0, 1), (2, 3)), ((0, 2), (1, 3)), ((0, 3), (1, 2))]
CROSS = 4
COUNTS = (len(INNER), CROSS)
PITCH = tuple(-(-2 * count // 8) * 8 for count in COUNTS)


def weight_tables():
    index = np.arange(N)
    angle = 2.0 * np.pi / N * (index[:, None] * index[None, :] % N)
    cos, sin = np.cos(angle), np.sin(angle)
    forward = np.block([[cos, sin], [-sin, cos]])
    tables = []
    for stage in (forward, forward.T):
        high = stage.astype(ml_dtypes.bfloat16)
        tables += [high, (stage - high.astype(np.float64)).astype(ml_dtypes.bfloat16)]
    return np.stack(tables)


def halves(value):
    high = value.astype(BF16)
    return high, (value - high.astype(F32)).astype(BF16)


def mm(a, b):
    return jnp.dot(a, b, preferred_element_type=F32)


def kernel(own, tables, out, wt, vis, kern, tot, part, take, send_f0, recv_f0, send_f1, recv_f1, send_b0, recv_b0,
           send_b1, recv_b1, table_sem, gather_send, gather_recv, pass_send, pass_recv, trans_send, trans_recv, local_sem,
           swap_send, swap_recv, give_send, give_recv, ready):
    band, slab = lax.axis_index("band"), lax.axis_index("slab")
    core, column = lax.rem(slab, 2), lax.div(slab, 2)
    z, x_hi = lax.rem(column, 8), lax.div(column, 8)
    y, x = lax.div(band, 2), x_hi * 2 + lax.rem(band, 2)
    home, slot = lax.div(band, 4), lax.rem(band, 4)
    me = column * 8 + band
    at = lambda b, s: {"band": b, "slab": s}
    sibling = at(band, column * 2 + 1 - core)

    load = pltpu.make_async_copy(tables, wt, table_sem)
    load.start()

    barrier = pltpu.get_barrier_semaphore()

    def greet_group(k, _):
        j = lax.rem(band * 2 + core + k, 16)
        pl.semaphore_signal(barrier, inc=1, device_id=at(lax.div(j, 2), column * 2 + lax.rem(j, 2)), device_id_type=MESH)
        return 0

    def greet_column(k, _):
        pl.semaphore_signal(barrier, inc=1, device_id=at(band, lax.rem(slab + 2 * k, 32)), device_id_type=MESH)
        return 0

    lax.fori_loop(1, 16, greet_group, 0)
    lax.fori_loop(1, 16, greet_column, 0)
    pl.semaphore_wait(barrier, 30)

    def gather(q):
        return pltpu.make_async_remote_copy(
            own.at[pl.ds(q * N, N)], vis.at[slot], gather_send.at[q], gather_recv.at[slot],
            device_id=at(4 * core + q, column * 2 + home), device_id_type=MESH)

    def keep(q):
        return pltpu.make_async_copy(own.at[pl.ds(q * N, N)], vis.at[slot], gather_recv.at[slot])

    stays = [jnp.logical_and(band == 4 * core + q, home == core) for q in range(4)]
    for q in range(4):
        pl.when(stays[q])(lambda q=q: keep(q).start())
        pl.when(jnp.logical_not(stays[q]))(lambda q=q: gather(q).start())

    def greet_ready(k, _):
        pl.semaphore_signal(ready, inc=1, device_id=at(lax.rem(band + k, 8), slab), device_id_type=MESH)
        return 0

    lax.fori_loop(1, 8, greet_ready, 0)

    fold = lambda v: jnp.where(v < N // 2, v, v - N).astype(F32)
    rows = lambda dim: lax.broadcasted_iota(jnp.int32, (N, N), dim)
    ky = fold(jnp.zeros((N, N), jnp.int32) + me)
    squared = fold(rows(0)) ** 2 + ky * ky + fold(rows(1)) ** 2
    scale = N**1.5 / 4.0 / float(N) ** 3
    kern[...] = jnp.where(squared > 0, scale / jnp.maximum(squared, 1.0), 0.0)
    tot[...] = jnp.zeros(tot.shape, F32)

    def left(stage, value):
        hi, lo = halves(value)
        return mm(wt[2 * stage], hi) + mm(wt[2 * stage], lo) + mm(wt[2 * stage + 1], hi)

    def right(value, stage):
        hi, lo = halves(value)
        return mm(hi, wt[2 * stage]) + mm(lo, wt[2 * stage]) + mm(hi, wt[2 * stage + 1])

    def wide(values):
        return jnp.concatenate(values, axis=1)

    def tall(values):
        return jnp.concatenate(values, axis=0)

    def put(ref, chunk, field):
        flat = ref.reshape(CHIPS * PITCH[chunk], N)
        for p in range(COUNTS[chunk]):
            for i in range(2):
                flat[pl.ds(2 * p + i, CHIPS, stride=PITCH[chunk]), :] = field[i * N:(i + 1) * N, p * N:(p + 1) * N]

    def get(ref, chunk):
        flat = ref.reshape(CHIPS * PITCH[chunk], N)
        return wide([tall([flat[pl.ds(2 * p + i, CHIPS, stride=PITCH[chunk]), :] for i in range(2)])
                     for p in range(COUNTS[chunk])])

    def analyse(pairs):
        spec = right(tall([wide([a, b]) for a, b in pairs]), 1)
        return left(0, wide([tall([spec[p * N:(p + 1) * N, :N], spec[p * N:(p + 1) * N, N:]]) for p in range(len(pairs))]))

    def convolve(columns):
        spec = left(0, columns)
        table = wide([kern[...]] * (columns.shape[1] // N))
        return left(1, tall([spec[:N] * table, spec[N:] * table]))

    def synthesise(columns):
        spec = left(1, columns)
        count = columns.shape[1] // N
        both = right(tall([wide([spec[:N, p * N:(p + 1) * N], spec[N:, p * N:(p + 1) * N]]) for p in range(count)]), 0)
        return [(both[p * N:(p + 1) * N, :N], both[p * N:(p + 1) * N, N:]) for p in range(count)]

    depths = [lax.rem(z + step, 8) for step in range(8)]

    def exchange(source, target, chunk, sem):
        used = pl.ds(0, 2 * COUNTS[chunk])

        def send(to_x, to_y, step):
            to_band, to_column = to_y * 2 + lax.rem(to_x, 2), lax.div(to_x, 2) * 8 + depths[step]
            pltpu.make_async_remote_copy(
                source.at[to_column * 8 + to_band, used], target.at[me, used], trans_send.at[sem], trans_recv.at[sem],
                device_id=at(to_band, to_column * 2 + core), device_id_type=MESH).start()

        def row(k, _):
            for step in (4, 3, 5, 2, 6, 1, 7, 0):
                send(lax.rem(x + lax.rem(k, 4), 4), lax.rem(y + lax.div(k, 4), 4), step)
            return 0

        lax.fori_loop(1, 16, row, 0)
        for step in (4, 3, 5, 2, 6, 1, 7):
            send(x, y, step)
        pltpu.make_async_copy(source.at[me, used], target.at[me, used], local_sem.at[sem]).start()

    def others(ref, chunk):
        return ref.at[pl.ds(0, CHIPS - 1), pl.ds(0, 2 * COUNTS[chunk])]

    def exchanged(source, target, chunk, sem):
        used = pl.ds(0, 2 * COUNTS[chunk])
        pltpu.make_async_copy(source.at[me, used], target.at[me, used], local_sem.at[sem]).wait()
        pltpu.make_async_copy(others(target, chunk), others(target, chunk), trans_recv.at[sem]).wait()

    def sent(source, chunk, sem):
        pltpu.make_async_copy(others(source, chunk), others(source, chunk), trans_send.at[sem]).wait()

    def hand_on(u):
        return pltpu.make_async_remote_copy(vis.at[u], vis.at[4 + u], pass_send.at[u], pass_recv.at[u],
                                            device_id=sibling, device_id_type=MESH)

    for u in range(4):
        pltpu.make_async_copy(vis.at[u], vis.at[u], gather_recv.at[u]).wait()
        hand_on(u).start()
    load.wait()
    put(send_f0, 0, analyse([tuple(vis[i] * vis[j] for i, j in pair) for pair in INNER]))
    pl.semaphore_wait(ready, 7)
    exchange(send_f0, recv_f0, 0, 0)

    for u in range(4):
        hand_on(u).wait_recv()
    across = [(u, 4 + lax.rem(core + u, 2)) for u in range(4)]
    put(send_f1, 1, analyse([(vis[u] * vis[v], vis[u] * vis[v + 2]) for u, v in across]))
    exchange(send_f1, recv_f1, 1, 1)

    exchanged(send_f0, recv_f0, 0, 0)
    put(send_b0, 0, convolve(get(recv_f0, 0)))
    exchange(send_b0, recv_b0, 0, 2)
    exchanged(send_f1, recv_f1, 1, 1)
    put(send_b1, 1, convolve(get(recv_f1, 1)))
    exchange(send_b1, recv_b1, 1, 3)

    exchanged(send_b0, recv_b0, 0, 2)
    for pair, fields in zip(INNER, synthesise(get(recv_b0, 0))):
        for (i, j), field in zip(pair, fields):
            tot[i] += field * vis[j]
            if i != j:
                tot[j] += field * vis[i]
    exchanged(send_b1, recv_b1, 1, 3)
    for (u, v), (first, second) in zip(across, synthesise(get(recv_b1, 1))):
        tot[u] += first * vis[v] + second * vis[v + 2]
        tot[v] += first * vis[u]
        tot[v + 2] += second * vis[u]

    def swap(u):
        return pltpu.make_async_remote_copy(tot.at[4 + u], part.at[u], swap_send.at[u], swap_recv.at[u],
                                            device_id=sibling, device_id_type=MESH)

    def give(u):
        return pltpu.make_async_remote_copy(
            part.at[u], take.at[pl.ds(slot * N, N)], give_send.at[u], give_recv.at[slot],
            device_id=at(4 * core + u, column * 2 + home), device_id_type=MESH)

    def keep_own(u):
        return pltpu.make_async_copy(part.at[u], take.at[pl.ds(slot * N, N)], give_recv.at[slot])

    for u in range(4):
        swap(u).start()
    for u in range(4):
        swap(u).wait_recv()
        part[u] = -0.25 * (part[u] + tot[u])
        pl.when(stays[u])(lambda u=u: keep_own(u).start())
        pl.when(jnp.logical_not(stays[u]))(lambda u=u: give(u).start())
    for q in range(4):
        block = take.at[pl.ds(q * N, N)]
        pltpu.make_async_copy(block, block, give_recv.at[q]).wait()
    out[...] = take[...]

    for q in range(4):
        pl.when(jnp.logical_not(stays[q]))(lambda q=q: gather(q).wait_send())
        pl.when(jnp.logical_not(stays[q]))(lambda q=q: give(q).wait_send())
        hand_on(q).wait_send()
        swap(q).wait_send()
    sent(send_f0, 0, 0)
    sent(send_f1, 1, 1)
    sent(send_b0, 0, 2)
    sent(send_b1, 1, 3)


def per_device(wavefunctions, tables):
    vmem, anywhere = pl.BlockSpec(memory_space=pltpu.VMEM), pl.BlockSpec(memory_space=pl.ANY)
    dma = pltpu.SemaphoreType.DMA
    chunks = [pltpu.VMEM((CHIPS, pitch, N), F32) for pitch in PITCH]
    planes = lambda count: pltpu.VMEM((count, N, N), F32)
    field = pl.pallas_call(
        kernel,
        out_shape=jax.ShapeDtypeStruct((4 * N, N), F32),
        in_specs=[anywhere, anywhere],
        out_specs=vmem,
        scratch_shapes=[
            pltpu.VMEM(tables.shape, BF16),
            planes(8), pltpu.VMEM((N, N), F32), planes(8), planes(4), pltpu.VMEM((4 * N, N), F32),
            chunks[0], chunks[0], chunks[1], chunks[1], chunks[0], chunks[0], chunks[1], chunks[1],
            dma, dma((4,)), dma((4,)), dma((4,)), dma((4,)), dma((4,)), dma((4,)), dma((4,)),
            dma((4,)), dma((4,)), dma((4,)), dma((4,)), pltpu.SemaphoreType.REGULAR,
        ],
        compiler_params=pltpu.CompilerParams(collective_id=0, has_side_effects=True, vmem_limit_bytes=48 << 20),
        name="exchange",
    )(wavefunctions.reshape(4 * N, N), tables)
    return field.reshape(1, 4, N, N)


def solution(mesh):
    tables = weight_tables()
    spec = P("band", "slab", None, None)
    run = jax.shard_map(per_device, mesh=mesh, in_specs=(spec, P()), out_specs=spec, check_vma=False)
    return lambda wavefunctions: run(wavefunctions, jnp.asarray(tables))
```

```python
import jax
import jax.numpy as jnp
import ml_dtypes
import numpy as np
from jax import lax
from jax.experimental import pallas as pl
from jax.experimental.pallas import tpu as pltpu
from jax.sharding import PartitionSpec as P

MESH = pl.DeviceIdType.MESH
N = 128
CHIPS = 128
BF16, F32 = jnp.bfloat16, jnp.float32

INNER = [((0, 0), (1, 1)), ((0, 1), (2, 3)), ((0, 2), (1, 3)), ((0, 3), (1, 2))]
LAST = [((2, 2), (3, 3))]
COUNTS = (len(INNER), 4, len(LAST))
PITCH = tuple(8 if count > 1 else 2 for count in COUNTS)


def weight_tables():
    index = np.arange(N)
    angle = 2.0 * np.pi / N * (index[:, None] * index[None, :] % N)
    cos, sin = np.cos(angle), np.sin(angle)
    forward = np.block([[cos, sin], [-sin, cos]])
    tables = []
    for stage in (forward, forward.T):
        high = stage.astype(ml_dtypes.bfloat16)
        tables += [high, (stage - high.astype(np.float64)).astype(ml_dtypes.bfloat16)]
    return np.stack(tables)


def halves(value):
    high = value.astype(BF16)
    return high, (value - high.astype(F32)).astype(BF16)


def mm(a, b):
    return jnp.dot(a, b, preferred_element_type=F32)


def kernel(own, tables, out, wt, vis, kern, tot, part, take, send_f0, recv_f0, send_f1, recv_f1, send_f2, recv_f2,
           send_b0, recv_b0, send_b1, recv_b1, send_b2, recv_b2, table_sem, gather_send, gather_recv, pass_send, pass_recv, trans_send, trans_recv, local_sem,
           swap_send, swap_recv, give_send, give_recv, ready):
    band, slab = lax.axis_index("band"), lax.axis_index("slab")
    core, column = lax.rem(slab, 2), lax.div(slab, 2)
    z, x_hi = lax.rem(column, 8), lax.div(column, 8)
    y, x = lax.div(band, 2), x_hi * 2 + lax.rem(band, 2)
    home, slot = lax.div(band, 4), lax.rem(band, 4)
    me = column * 8 + band
    at = lambda b, s: {"band": b, "slab": s}
    sibling = at(band, column * 2 + 1 - core)

    load = pltpu.make_async_copy(tables, wt, table_sem)
    load.start()

    barrier = pltpu.get_barrier_semaphore()

    def greet_group(k, _):
        j = lax.rem(band * 2 + core + k, 16)
        pl.semaphore_signal(barrier, inc=1, device_id=at(lax.div(j, 2), column * 2 + lax.rem(j, 2)), device_id_type=MESH)
        return 0

    def greet_column(k, _):
        pl.semaphore_signal(barrier, inc=1, device_id=at(band, lax.rem(slab + 2 * k, 32)), device_id_type=MESH)
        return 0

    lax.fori_loop(1, 16, greet_group, 0)
    lax.fori_loop(1, 16, greet_column, 0)
    pl.semaphore_wait(barrier, 30)

    turned = [lax.rem(slot + i, 4) for i in range(4)]
    stays = home == core

    def gather(i):
        return pltpu.make_async_remote_copy(
            own.at[pl.ds(turned[i] * N, N)], vis.at[slot], gather_send.at[i], gather_recv.at[slot],
            device_id=at(4 * core + turned[i], column * 2 + home), device_id_type=MESH)

    def unless_stays(remote, local):
        pl.when(stays)(lambda: local.start())
        pl.when(jnp.logical_not(stays))(lambda: remote.start())

    for i in range(1, 4):
        gather(i).start()
    unless_stays(gather(0), pltpu.make_async_copy(own.at[pl.ds(slot * N, N)], vis.at[slot], gather_recv.at[slot]))

    def greet_ready(k, _):
        pl.semaphore_signal(ready, inc=1, device_id=at(lax.rem(band + k, 8), slab), device_id_type=MESH)
        return 0

    lax.fori_loop(1, 8, greet_ready, 0)

    fold = lambda v: jnp.where(v < N // 2, v, v - N).astype(F32)
    rows = lambda dim: lax.broadcasted_iota(jnp.int32, (N, N), dim)
    ky = fold(jnp.zeros((N, N), jnp.int32) + me)
    squared = fold(rows(0)) ** 2 + ky * ky + fold(rows(1)) ** 2
    scale = N**1.5 / 4.0 / float(N) ** 3
    kern[...] = jnp.where(squared > 0, scale / jnp.maximum(squared, 1.0), 0.0)
    tot[...] = jnp.zeros(tot.shape, F32)

    def left(stage, value):
        hi, lo = halves(value)
        return mm(wt[2 * stage], hi) + mm(wt[2 * stage], lo) + mm(wt[2 * stage + 1], hi)

    def right(value, stage):
        hi, lo = halves(value)
        return mm(hi, wt[2 * stage]) + mm(lo, wt[2 * stage]) + mm(hi, wt[2 * stage + 1])

    def wide(values):
        return jnp.concatenate(values, axis=1)

    def tall(values):
        return jnp.concatenate(values, axis=0)

    def put(ref, chunk, field):
        flat = ref.reshape(CHIPS * PITCH[chunk], N)
        for p in range(COUNTS[chunk]):
            for i in range(2):
                flat[pl.ds(2 * p + i, CHIPS, stride=PITCH[chunk]), :] = field[i * N:(i + 1) * N, p * N:(p + 1) * N]

    def get(ref, chunk):
        flat = ref.reshape(CHIPS * PITCH[chunk], N)
        return wide([tall([flat[pl.ds(2 * p + i, CHIPS, stride=PITCH[chunk]), :] for i in range(2)])
                     for p in range(COUNTS[chunk])])

    def analyse(pairs):
        spec = right(tall([wide([a, b]) for a, b in pairs]), 1)
        return left(0, wide([tall([spec[p * N:(p + 1) * N, :N], spec[p * N:(p + 1) * N, N:]]) for p in range(len(pairs))]))

    def convolve(columns):
        spec = left(0, columns)
        table = wide([kern[...]] * (columns.shape[1] // N))
        return left(1, tall([spec[:N] * table, spec[N:] * table]))

    def synthesise(columns):
        spec = left(1, columns)
        count = columns.shape[1] // N
        both = right(tall([wide([spec[:N, p * N:(p + 1) * N], spec[N:, p * N:(p + 1) * N]]) for p in range(count)]), 0)
        return [(both[p * N:(p + 1) * N, :N], both[p * N:(p + 1) * N, N:]) for p in range(count)]

    depths = [lax.rem(z + step, 8) for step in range(8)]

    def exchange(source, target, chunk, sem):
        used = pl.ds(0, 2 * COUNTS[chunk])

        def send(to_x, to_y, step):
            to_band, to_column = to_y * 2 + lax.rem(to_x, 2), lax.div(to_x, 2) * 8 + depths[step]
            pltpu.make_async_remote_copy(
                source.at[to_column * 8 + to_band, used], target.at[me, used], trans_send.at[sem], trans_recv.at[sem],
                device_id=at(to_band, to_column * 2 + core), device_id_type=MESH).start()

        def row(k, _):
            for step in (4, 3, 5, 2, 6, 1, 7, 0):
                send(lax.rem(x + lax.rem(k, 4), 4), lax.rem(y + lax.div(k, 4), 4), step)
            return 0

        lax.fori_loop(1, 16, row, 0)
        for step in (4, 3, 5, 2, 6, 1, 7):
            send(x, y, step)
        pltpu.make_async_copy(source.at[me, used], target.at[me, used], local_sem.at[sem]).start()

    def others(ref, chunk):
        return ref.at[pl.ds(0, CHIPS - 1), pl.ds(0, 2 * COUNTS[chunk])]

    def exchanged(source, target, chunk, sem):
        used = pl.ds(0, 2 * COUNTS[chunk])
        pltpu.make_async_copy(source.at[me, used], target.at[me, used], local_sem.at[sem]).wait()
        pltpu.make_async_copy(others(target, chunk), others(target, chunk), trans_recv.at[sem]).wait()

    def sent(source, chunk, sem):
        pltpu.make_async_copy(others(source, chunk), others(source, chunk), trans_send.at[sem]).wait()

    def hand_on(u):
        return pltpu.make_async_remote_copy(vis.at[u], vis.at[4 + u], pass_send.at[u], pass_recv.at[u],
                                            device_id=sibling, device_id_type=MESH)

    for u in range(4):
        pltpu.make_async_copy(vis.at[u], vis.at[u], gather_recv.at[u]).wait()
        hand_on(u).start()
    load.wait()
    put(send_f0, 0, analyse([tuple(vis[i] * vis[j] for i, j in pair) for pair in INNER]))
    pl.semaphore_wait(ready, 7)
    exchange(send_f0, recv_f0, 0, 0)

    for u in range(4):
        hand_on(u).wait_recv()
    across = [(u, 4 + lax.rem(core + u, 2)) for u in range(4)]
    put(send_f1, 1, analyse([(vis[u] * vis[v], vis[u] * vis[v + 2]) for u, v in across]))
    exchange(send_f1, recv_f1, 1, 1)
    put(send_f2, 2, analyse([tuple(vis[i] * vis[j] for i, j in pair) for pair in LAST]))
    exchange(send_f2, recv_f2, 2, 2)

    exchanged(send_f0, recv_f0, 0, 0)
    put(send_b0, 0, convolve(get(recv_f0, 0)))
    exchange(send_b0, recv_b0, 0, 3)
    exchanged(send_f1, recv_f1, 1, 1)
    put(send_b1, 1, convolve(get(recv_f1, 1)))
    exchange(send_b1, recv_b1, 1, 4)
    exchanged(send_f2, recv_f2, 2, 2)
    put(send_b2, 2, convolve(get(recv_f2, 2)))
    exchange(send_b2, recv_b2, 2, 5)

    def collect(pairs, columns):
        for pair, fields in zip(pairs, synthesise(columns)):
            for (i, j), field in zip(pair, fields):
                tot[i] += field * vis[j]
                if i != j:
                    tot[j] += field * vis[i]

    exchanged(send_b0, recv_b0, 0, 3)
    collect(INNER, get(recv_b0, 0))
    exchanged(send_b1, recv_b1, 1, 4)
    for (u, v), (first, second) in zip(across, synthesise(get(recv_b1, 1))):
        tot[u] += first * vis[v] + second * vis[v + 2]
        tot[v] += first * vis[u]
        tot[v + 2] += second * vis[u]

    def swap(u):
        return pltpu.make_async_remote_copy(tot.at[4 + u], part.at[u], swap_send.at[u], swap_recv.at[u],
                                            device_id=sibling, device_id_type=MESH)

    mine = take.at[pl.ds(slot * N, N)]

    def give(u):
        return pltpu.make_async_remote_copy(
            part.at[u], mine, give_send.at[u], give_recv.at[slot],
            device_id=at(4 * core + u, column * 2 + home), device_id_type=MESH)

    def finish(u):
        part[u] = -0.25 * (part[u] + tot[u])
        here = jnp.logical_and(stays, slot == u)
        pl.when(here)(lambda: pltpu.make_async_copy(part.at[u], mine, give_recv.at[slot]).start())
        pl.when(jnp.logical_not(here))(lambda: give(u).start())

    for u in range(4):
        swap(u).start()
    for u in range(4):
        swap(u).wait_recv()
    flip = lax.rem(slot, 2)
    finish(flip)
    finish(1 - flip)
    exchanged(send_b2, recv_b2, 2, 5)
    collect(LAST, get(recv_b2, 2))
    finish(2 + flip)
    finish(3 - flip)
    for q in range(4):
        block = take.at[pl.ds(q * N, N)]
        pltpu.make_async_copy(block, block, give_recv.at[q]).wait()
    out[...] = take[...]

    for q in range(4):
        if q == 0:
            pl.when(jnp.logical_not(stays))(lambda: gather(0).wait_send())
        else:
            gather(q).wait_send()
        pl.when(jnp.logical_not(jnp.logical_and(stays, slot == q)))(lambda q=q: give(q).wait_send())
        hand_on(q).wait_send()
        swap(q).wait_send()
    sent(send_f0, 0, 0)
    sent(send_f1, 1, 1)
    sent(send_f2, 2, 2)
    sent(send_b0, 0, 3)
    sent(send_b1, 1, 4)
    sent(send_b2, 2, 5)


def per_device(wavefunctions, tables):
    vmem, far = pl.BlockSpec(memory_space=pltpu.VMEM), pl.BlockSpec(memory_space=pltpu.HBM)
    dma = pltpu.SemaphoreType.DMA
    chunks = [pltpu.VMEM((CHIPS, pitch, N), F32) for pitch in PITCH]
    planes = lambda count: pltpu.VMEM((count, N, N), F32)
    field = pl.pallas_call(
        kernel,
        out_shape=jax.ShapeDtypeStruct((4 * N, N), F32),
        in_specs=[far, far],
        out_specs=vmem,
        scratch_shapes=[
            pltpu.VMEM(tables.shape, BF16),
            planes(8), pltpu.VMEM((N, N), F32), planes(8), planes(4), pltpu.VMEM((4 * N, N), F32),
            *[chunk for chunk in chunks * 2 for _ in range(2)],
            dma, dma((4,)), dma((4,)), dma((4,)), dma((4,)), dma((6,)), dma((6,)), dma((6,)),
            dma((4,)), dma((4,)), dma((4,)), dma((4,)), pltpu.SemaphoreType.REGULAR,
        ],
        compiler_params=pltpu.CompilerParams(collective_id=0, has_side_effects=True, vmem_limit_bytes=48 << 20),
        name="exchange",
    )(*[pltpu.with_memory_space_constraint(value, pltpu.HBM) for value in (wavefunctions.reshape(4 * N, N), tables)])
    return field.reshape(1, 4, N, N)


def solution(mesh):
    tables = weight_tables()
    spec = P("band", "slab", None, None)
    run = jax.shard_map(per_device, mesh=mesh, in_specs=(spec, P()), out_specs=spec, check_vma=False)
    return lambda wavefunctions: run(wavefunctions, jnp.asarray(tables))
```

```python
import jax
import jax.numpy as jnp
import ml_dtypes
import numpy as np
from jax import lax
from jax.experimental import pallas as pl
from jax.experimental.pallas import tpu as pltpu
from jax.sharding import PartitionSpec as P

MESH = pl.DeviceIdType.MESH
N = 128
PEERS = 32
USED, PITCH = 18, 24
BF16, F32 = jnp.bfloat16, jnp.float32
FWD, INV, Y_FWD, Y_INV, HALF_FWD, HALF_INV = range(6)

HELD = (0, 1, 3, 4)
ROUTES = (
    ((0, 7), (7, 5), (5, 4)),
    ((0, 1), (0, 6), (6, 5)),
    ((0, 1), (1, 2), (0, 7), (7, 6)),
    ((0, 2), (2, 3), (0, 7)),
    ((0, 1), (1, 3), (3, 4)),
    ((0, 1), (1, 2), (0, 5), (5, 4)),
    ((0, 2), (2, 3), (0, 6), (6, 5)),
    ((0, 3), (3, 4), (0, 7), (7, 6)),
)


def stride_of(start, end):
    return end - start if start <= end <= 4 and start < 4 else end - (start or 8)


def source_core(r):
    return 0 if r in HELD else 1


def place(distance, r):
    if distance == 0:
        return source_core(r), 0
    return (0, distance) if distance < 4 else (1, 7 - distance)


def starts_at(distance, r):
    return [end for start, end in ROUTES[r] if start == distance]


def weight_tables():
    index = np.arange(N)
    angle = 2.0 * np.pi / N * (index[:, None] * index[None, :] % N)
    cos, sin = np.cos(angle), np.sin(angle)
    forward = np.block([[cos, sin], [-sin, cos]])
    sign = 1.0 - 2.0 * (index % 2)
    ones = np.ones(N)

    def order(width):
        peer, part, sub = np.meshgrid(np.arange(PEERS), np.arange(2), np.arange(width), indexing="ij")
        return (part * N + peer * width + sub).reshape(-1)

    half_forward = forward.copy()
    half_forward[0] = np.concatenate([ones, -sign])
    half_forward[N] = np.concatenate([sign, ones])
    half_inverse = 2.0 * forward.T
    half_inverse[:, 0] = np.concatenate([ones, -sign])
    half_inverse[:, N] = np.concatenate([sign, ones])
    pad = np.zeros((2 * N, 2 * N))
    half_fwd, half_inv = pad.copy(), pad.copy()
    half_fwd[:N] = half_forward[order(2)]
    half_inv[:, :N] = half_inverse[:, order(2)]
    y_fwd = forward[order(4)]
    tables = []
    for stage in (forward, forward.T, y_fwd, y_fwd.T, half_fwd, half_inv):
        high = stage.astype(ml_dtypes.bfloat16)
        tables += [high, (stage - high.astype(np.float64)).astype(ml_dtypes.bfloat16)]
    return np.stack(tables)


def halves(value):
    high = value.astype(BF16)
    return high, (value - high.astype(F32)).astype(BF16)


def mm(a, b):
    return jnp.dot(a, b, preferred_element_type=F32)


def wide(values):
    return jnp.concatenate(values, axis=1)


def tall(values):
    return jnp.concatenate(values, axis=0)


def kernel(own, tables, out, wt, vis, kern, part, inner, plus, minus, take, half_out, half_in, send_f, recv_f, send_b, recv_b,
           table_sem, gather_send, vis_recv, relay_send, f_send, f_recv, f_local, b_send, b_recv, b_local, sum_send, inner_recv,
           plus_recv, minus_recv, give_send, give_recv):
    band, slab = lax.axis_index("band"), lax.axis_index("slab")
    core, column = lax.rem(slab, 2), lax.div(slab, 2)
    z, x_hi = lax.rem(column, 8), lax.div(column, 8)
    y, x = lax.div(band, 2), x_hi * 2 + lax.rem(band, 2)
    home, slot, half = lax.div(band, 4), lax.rem(band, 4), lax.div(z, 4)
    me = (x_hi * 8 + band) * 2 + core
    lower = core == 0
    at = lambda b, s: {"band": b, "slab": s}

    def layer(step, to_core):
        return at(band, (x_hi * 8 + lax.rem(z + step + 8, 8)) * 2 + to_core)

    load = pltpu.make_async_copy(tables, wt, table_sem)
    load.start()

    barrier = pltpu.get_barrier_semaphore()

    def greet_layer(k, _):
        j = lax.rem(me + k, PEERS)
        b, c = lax.rem(lax.div(j, 2), 8), lax.rem(j, 2)
        pl.semaphore_signal(barrier, inc=1, device_id=at(b, (lax.div(j, 16) * 8 + z) * 2 + c), device_id_type=MESH)
        return 0

    def greet_pillar(k, _):
        pl.semaphore_signal(barrier, inc=1, device_id=layer(lax.div(k, 2), lax.rem(k, 2)), device_id_type=MESH)
        return 0

    lax.fori_loop(1, PEERS, greet_layer, 0)
    lax.fori_loop(2, 16, greet_pillar, 0)
    pl.semaphore_wait(barrier, PEERS - 1 + 14)

    turned = [lax.rem(slot + i, 4) for i in range(4)]
    rank = lax.rem(band - z + 8, 8)
    in_held = sum(jnp.where(rank == e, 1, 0) for e in HELD)
    collector = 1 - in_held
    stays = jnp.logical_and(home == core, collector == core)

    def gather(i):
        return pltpu.make_async_remote_copy(
            own.at[pl.ds(turned[i] * N, N)], vis.at[0, rank], gather_send.at[i], vis_recv.at[0, rank],
            device_id=at(4 * core + turned[i], column * 2 + collector), device_id_type=MESH)

    for i in range(1, 4):
        gather(i).start()
    keep = pltpu.make_async_copy(own.at[pl.ds(slot * N, N)], vis.at[0, rank], vis_recv.at[0, rank])
    pl.when(stays)(lambda: keep.start())
    pl.when(jnp.logical_not(stays))(lambda: gather(0).start())

    fold = lambda v: jnp.where(v < N // 2, v, v - N).astype(F32)
    line = lambda dim: lax.broadcasted_iota(jnp.int32, (N, N), dim)
    plane_sq = fold(line(0)) ** 2 + fold(line(1)) ** 2
    scale = N**1.5 / 4.0 / float(N) ** 3

    def coulomb(row):
        ky = fold(jnp.zeros((N, N), jnp.int32) + row)
        squared = plane_sq + ky * ky
        return jnp.where(squared > 0, scale / jnp.maximum(squared, 1.0), 0.0)

    for j in range(4):
        kern[j] = coulomb((x_hi * 8 + band) * 8 + core * 4 + j)
    row = 2 * me + half
    special = jnp.zeros((N, N), jnp.int32) + row == 0
    plain, nyquist = coulomb(row), coulomb(N // 2)
    kern[4] = jnp.where(special, 0.5 * (plain + nyquist), plain)
    kern[5] = jnp.where(special, 0.5 * (plain - nyquist), 0.0)
    flipped = jnp.where(lax.rem(line(0) + line(1), N) == 0, 1.0, 0.0).astype(BF16)
    half_in[...] = jnp.zeros(half_in.shape, F32)

    def left(stage, value, rows=2 * N, depth=2 * N):
        hi, lo = halves(value)
        high, low = wt[2 * stage, :rows, :depth], wt[2 * stage + 1, :rows, :depth]
        return mm(high, hi) + mm(high, lo) + mm(low, hi)

    def right(value, stage):
        hi, lo = halves(value)
        return mm(hi, wt[2 * stage]) + mm(lo, wt[2 * stage]) + mm(hi, wt[2 * stage + 1])

    def distance(k, of_core):
        return k + of_core * (7 - 2 * k)

    def plane_index(of_x_hi, of_band, k, of_core):
        return of_x_hi * 64 + lax.rem(z - distance(k, of_core) + 8, 8) * 8 + of_band

    def chips(visit):
        def step(k, _):
            to_x, to_y = lax.rem(x + lax.rem(k, 4), 4), lax.rem(y + lax.div(k, 4), 4)
            visit(lax.div(to_x, 2), to_y * 2 + lax.rem(to_x, 2))
            return 0
        lax.fori_loop(1, 16, step, 0)

    used = pl.ds(0, USED)

    def send_plane(k):
        mine = plane_index(x_hi, band, k, core)

        def visit(to_x_hi, to_band, to_core):
            pltpu.make_async_remote_copy(
                send_f.at[k, (to_x_hi * 8 + to_band) * 2 + to_core, used], recv_f.at[mine, used], f_send, f_recv,
                device_id=at(to_band, (to_x_hi * 8 + z) * 2 + to_core), device_id_type=MESH).start()

        chips(lambda *chip: [visit(*chip, to_core) for to_core in range(2)])
        visit(x_hi, band, 1 - core)
        pltpu.make_async_copy(send_f.at[k, me, used], recv_f.at[mine, used], f_local.at[k]).start()

    def return_planes(*planes):
        def visit(to_x_hi, to_band):
            for to_core, k in planes:
                pltpu.make_async_remote_copy(
                    send_b.at[plane_index(to_x_hi, to_band, k, to_core), used], recv_b.at[k, me, used], b_send, b_recv.at[k],
                    device_id=at(to_band, (to_x_hi * 8 + z) * 2 + to_core), device_id_type=MESH).start()

        chips(visit)
        for to_core, k in planes:
            @pl.when(core == to_core)
            def _():
                pltpu.make_async_copy(send_b.at[plane_index(x_hi, band, k, to_core), used], recv_b.at[k, me, used],
                                      b_local.at[k]).start()

            @pl.when(core != to_core)
            def _():
                pltpu.make_async_remote_copy(
                    send_b.at[plane_index(x_hi, band, k, to_core), used], recv_b.at[k, me, used], b_send, b_recv.at[k],
                    device_id=at(band, column * 2 + to_core), device_id_type=MESH).start()

    def arrived(k, e):
        pltpu.make_async_copy(vis.at[k, e], vis.at[k, e], vis_recv.at[k, e]).wait()

    def pass_on(here, k, r):
        for end in starts_at(here, r):
            to_core, to_k = place(end, r)
            source, target = (r - here) % 8, (r - end) % 8
            pltpu.make_async_remote_copy(
                vis.at[k, source], vis.at[to_k, target], relay_send, vis_recv.at[to_k, target],
                device_id=layer(stride_of(here, end), to_core), device_id_type=MESH).start()

    def start_plane(of_core, k):
        if k == 0:
            for r in (0, 4, 3, 1) if of_core == 0 else (7, 5, 2, 6):
                arrived(0, r)
                pass_on(0, 0, r)
        here = distance(k, of_core)
        ranks = [(here + e) % 8 for e in HELD]
        if here:
            for r in sorted(ranks, key=lambda r: -len(starts_at(here, r))):
                arrived(k, (r - here) % 8)
                pass_on(here, k, r)

    def analyse(k):
        f0, f1, f3, f4 = [vis[k, e] for e in HELD]
        fields = [f0 * f0, f0 * f1, f1 * f3, f0 * f3, f0 * f4, jnp.zeros((N, N), F32)]
        spec = right(tall([wide(fields[2 * p:2 * p + 2]) for p in range(3)]), INV)
        stacked = [tall([spec[p * N:(p + 1) * N, :N], spec[p * N:(p + 1) * N, N:]]) for p in range(3)]
        full = left(Y_FWD, wide(stacked[:2]))
        for p in range(2):
            send_f[k, :, 8 * p:8 * p + 8, :] = full[:, p * N:(p + 1) * N].reshape(PEERS, 8, N)
        half_out[...] = left(HALF_FWD, stacked[2], rows=N)
        flat = send_f.reshape(4 * PEERS * PITCH, N)
        for i in range(2):
            flat[pl.ds(k * PEERS * PITCH + 16 + i, PEERS, stride=PITCH), :] = half_out[pl.ds(2 * i + half, PEERS, stride=4), :]

    for k in range(4):
        pl.when(lower)(lambda k=k: start_plane(0, k))
        pl.when(jnp.logical_not(lower))(lambda k=k: start_plane(1, k))
        if k == 0:
            load.wait()
        analyse(k)
        send_plane(k)

    flat_f, flat_b = recv_f.reshape(N * PITCH, N), send_b.reshape(N * PITCH, N)
    for k in range(4):
        mine = plane_index(x_hi, band, k, core)
        pltpu.make_async_copy(send_f.at[k, me, used], recv_f.at[mine, used], f_local.at[k]).wait()
    arrivals = recv_f.at[pl.ds(0, 4 * (PEERS - 1)), used]
    pltpu.make_async_copy(arrivals, arrivals, f_recv).wait()

    def strip(r):
        return flat_f[pl.ds(r, N, stride=PITCH), :]

    def store(r, value):
        flat_b[pl.ds(r, N, stride=PITCH), :] = value

    for p in range(2):
        spec = left(FWD, wide([tall([strip(8 * p + j), strip(8 * p + 4 + j)]) for j in range(4)]))
        table = wide([kern[j] for j in range(4)])
        field = left(INV, tall([spec[:N] * table, spec[N:] * table]))
        for j in range(4):
            store(8 * p + j, field[:N, j * N:(j + 1) * N])
            store(8 * p + 4 + j, field[N:, j * N:(j + 1) * N])
    real, imag = strip(16), strip(17)
    hi, lo = halves(tall([real, -imag]))
    spec = left(FWD, wide([tall([real, imag]), mm(hi, flipped) + mm(lo, flipped)]))
    field = left(INV, tall([spec[i * N:(i + 1) * N, :N] * kern[4] + spec[i * N:(i + 1) * N, N:] * kern[5] for i in range(2)]))
    store(16, field[:N])
    store(17, field[N:])
    return_planes((1, 3))
    for k in (3, 2, 1):
        return_planes((0, k), (1, k - 1))
    return_planes((0, 0))

    def synthesise(k):
        mine = plane_index(x_hi, band, k, core)
        pltpu.make_async_copy(send_b.at[mine, used], recv_b.at[k, me, used], b_local.at[k]).wait()
        block = recv_b.at[k, pl.ds(0, PEERS - 1), used]
        pltpu.make_async_copy(block, block, b_recv.at[k]).wait()
        full = left(Y_INV, wide([recv_b[k, :, 8 * p:8 * p + 8, :].reshape(2 * N, N) for p in range(2)]))
        flat = recv_b.reshape(4 * PEERS * PITCH, N)
        for i in range(2):
            half_in[pl.ds(2 * i + half, PEERS, stride=4), :] = flat[pl.ds(k * PEERS * PITCH + 16 + i, PEERS, stride=PITCH), :]
        spec = [full[:, :N], full[:, N:], left(HALF_INV, half_in[...], depth=N)]
        both = right(tall([wide([s[:N], s[N:]]) for s in spec]), FWD)
        fields = [both[(e // 2) * N:(e // 2 + 1) * N, (e % 2) * N:(e % 2 + 1) * N] for e in range(5)]
        f0, f1, f3, f4 = [vis[k, e] for e in HELD]
        part[k, 0] = fields[0] * f0 + fields[1] * f1 + fields[3] * f3 + fields[4] * f4
        part[k, 1] = fields[1] * f0 + fields[2] * f3
        part[k, 3] = fields[2] * f1 + fields[3] * f0
        part[k, 4] = fields[4] * f0

    def pass_sums(of_core, k):
        here = distance(k, of_core)
        ranks = [(here + e) % 8 for e in HELD]
        for r in sorted(ranks, key=lambda r: len(starts_at(here, r))):
            e = (r - here) % 8
            if starts_at(here, r):
                pltpu.make_async_copy(inner.at[k, e], inner.at[k, e], inner_recv.at[k, e]).wait()
                part[k, e] += inner[k, e]
            (back,) = [start for start, end in ROUTES[r] if end == here]
            step = stride_of(back, here)
            to_core, to_k = place(back, r)
            to_e = (r - back) % 8
            target, sem = (inner, inner_recv) if back else (plus, plus_recv) if step > 0 else (minus, minus_recv)
            index = (to_k, to_e) if back else (r,)
            pltpu.make_async_remote_copy(part.at[k, e], target.at[index], sum_send, sem.at[index],
                                         device_id=layer(-step, to_core), device_id_type=MESH).start()

    for k in (3, 2, 1, 0):
        synthesise(k)
        if k:
            pl.when(lower)(lambda k=k: pass_sums(0, k))
        pl.when(jnp.logical_not(lower))(lambda k=k: pass_sums(1, k))

    mine = take.at[pl.ds(slot * N, N)]

    def give(r):
        return pltpu.make_async_remote_copy(part.at[0, r], mine, give_send.at[r], give_recv.at[slot],
                                            device_id=at(lax.rem(z + r, 8), column * 2 + home), device_id_type=MESH)

    def keeps(r):
        return jnp.logical_and(home == core, rank == r)

    def finish(ranks):
        for r in ranks:
            total = part[0, r] if r in HELD else None
            strides = [stride_of(0, end) for end in starts_at(0, r)]
            for ref, sem, sign in ((plus, plus_recv, 1), (minus, minus_recv, -1)):
                if any(step * sign > 0 for step in strides):
                    pltpu.make_async_copy(ref.at[r], ref.at[r], sem.at[r]).wait()
                    total = ref[r] if total is None else total + ref[r]
            part[0, r] = -0.25 * total
            pl.when(keeps(r))(lambda r=r: pltpu.make_async_copy(part.at[0, r], mine, give_recv.at[slot]).start())
            pl.when(jnp.logical_not(keeps(r)))(lambda r=r: give(r).start())

    pl.when(lower)(lambda: finish((4, 1, 0, 3)))
    pl.when(jnp.logical_not(lower))(lambda: finish((5, 6, 7, 2)))

    for q in range(4):
        block = take.at[pl.ds(q * N, N)]
        pltpu.make_async_copy(block, block, give_recv.at[q]).wait()
    out[...] = take[...]

    for i in range(1, 4):
        gather(i).wait_send()
    pl.when(jnp.logical_not(stays))(lambda: gather(0).wait_send())
    for sem, source in ((f_send, recv_f), (b_send, send_b)):
        block = source.at[pl.ds(0, 4 * (PEERS - 1)), used]
        pltpu.make_async_copy(block, block, sem).wait()

    def left_by(sem, ref, count):
        block = ref.reshape(32 * N, N).at[pl.ds(0, count * N)]
        pltpu.make_async_copy(block, block, sem).wait()

    def settle(ranks, relays, sums):
        left_by(relay_send, vis, relays)
        left_by(sum_send, part, sums)
        for r in ranks:
            pl.when(jnp.logical_not(keeps(r)))(lambda r=r: give(r).wait_send())

    pl.when(lower)(lambda: settle((0, 1, 3, 4), 13, 12))
    pl.when(jnp.logical_not(lower))(lambda: settle((2, 5, 6, 7), 15, 16))


def per_device(wavefunctions, tables):
    dma = pltpu.SemaphoreType.DMA
    planes = lambda *shape: pltpu.VMEM((*shape, N, N), F32)
    by_peer, by_plane = pltpu.VMEM((4, PEERS, PITCH, N), F32), pltpu.VMEM((N, PITCH, N), F32)
    field = pl.pallas_call(
        kernel,
        out_shape=jax.ShapeDtypeStruct((4 * N, N), F32),
        in_specs=[pl.BlockSpec(memory_space=pltpu.HBM)] * 2,
        out_specs=pl.BlockSpec(memory_space=pltpu.VMEM),
        scratch_shapes=[
            pltpu.VMEM(tables.shape, BF16), planes(4, 8), planes(6), planes(4, 8), planes(4, 8), planes(8), planes(8),
            pltpu.VMEM((4 * N, N), F32), planes(), planes(), by_peer, by_plane, by_plane, by_peer,
            dma, dma((4,)), dma((4, 8)), dma, dma, dma, dma((4,)), dma, dma((4,)), dma((4,)), dma, dma((4, 8)),
            dma((8,)), dma((8,)), dma((8,)), dma((4,)),
        ],
        compiler_params=pltpu.CompilerParams(collective_id=0, has_side_effects=True, vmem_limit_bytes=48 << 20),
        name="exchange",
    )(*[pltpu.with_memory_space_constraint(value, pltpu.HBM) for value in (wavefunctions.reshape(4 * N, N), tables)])
    return field.reshape(1, 4, N, N)


def solution(mesh):
    tables = weight_tables()
    spec = P("band", "slab", None, None)
    run = jax.shard_map(per_device, mesh=mesh, in_specs=(spec, P()), out_specs=spec, check_vma=False)
    return lambda wavefunctions: run(wavefunctions, jnp.asarray(tables))
```

```python
import jax
import jax.numpy as jnp
import ml_dtypes
import numpy as np
from jax import lax
from jax.experimental import pallas as pl
from jax.experimental.pallas import tpu as pltpu
from jax.sharding import PartitionSpec as P

MESH = pl.DeviceIdType.MESH
N = 128
PEERS = 32
USED, PITCH = 18, 24
BF16, F32 = jnp.bfloat16, jnp.float32
FWD, INV, Y_FWD, Y_INV, HALF_FWD, HALF_INV = range(6)

HELD = (0, 1, 3, 4)
ROUTES = (
    ((0, 7), (7, 5), (5, 4)),
    ((0, 1), (0, 6), (6, 5)),
    ((0, 1), (1, 2), (0, 7), (7, 6)),
    ((0, 2), (2, 3), (0, 7)),
    ((0, 1), (1, 3), (3, 4)),
    ((0, 1), (1, 2), (0, 5), (5, 4)),
    ((0, 2), (2, 3), (0, 6), (6, 5)),
    ((0, 3), (3, 4), (0, 7), (7, 6)),
)


def stride_of(start, end):
    return end - start if start <= end <= 4 and start < 4 else end - (start or 8)


def source_core(r):
    return 0 if r in HELD else 1


def place(distance, r):
    if distance == 0:
        return source_core(r), 0
    return (0, distance) if distance < 4 else (1, 7 - distance)


def starts_at(distance, r):
    return [end for start, end in ROUTES[r] if start == distance]


def sides(r):
    strides = [stride_of(0, end) for end in starts_at(0, r)]
    return [side for side, present in enumerate((max(strides) > 0, min(strides) < 0, r in HELD)) if present]


def weight_tables():
    index = np.arange(N)
    angle = 2.0 * np.pi / N * (index[:, None] * index[None, :] % N)
    cos, sin = np.cos(angle), np.sin(angle)
    forward = np.block([[cos, sin], [-sin, cos]])
    sign = 1.0 - 2.0 * (index % 2)
    ones = np.ones(N)

    def order(width):
        peer, part, sub = np.meshgrid(np.arange(PEERS), np.arange(2), np.arange(width), indexing="ij")
        return (part * N + peer * width + sub).reshape(-1)

    half_forward = forward.copy()
    half_forward[0] = np.concatenate([ones, -sign])
    half_forward[N] = np.concatenate([sign, ones])
    half_inverse = 2.0 * forward.T
    half_inverse[:, 0] = np.concatenate([ones, -sign])
    half_inverse[:, N] = np.concatenate([sign, ones])
    pad = np.zeros((2 * N, 2 * N))
    half_fwd, half_inv = pad.copy(), pad.copy()
    half_fwd[:N] = half_forward[order(2)]
    half_inv[:, :N] = half_inverse[:, order(2)]
    y_fwd = forward[order(4)]
    tables = []
    for stage in (forward, forward.T, y_fwd, y_fwd.T, half_fwd, half_inv):
        high = stage.astype(ml_dtypes.bfloat16)
        tables += [high, (stage - high.astype(np.float64)).astype(ml_dtypes.bfloat16)]
    return np.stack(tables)


def halves(value):
    high = value.astype(BF16)
    return high, (value - high.astype(F32)).astype(BF16)


def mm(a, b):
    return jnp.dot(a, b, preferred_element_type=F32)


def wide(values):
    return jnp.concatenate(values, axis=1)


def tall(values):
    return jnp.concatenate(values, axis=0)


def kernel(own, tables, out, wt, vis, kern, part, inner, arrive, half_out, half_in, send_f, recv_f, send_b, recv_b,
           table_sem, gather_send, vis_recv, relay_send, f_send, f_recv, f_local, b_send, b_recv, b_local, sum_send, inner_recv,
           arrive_recv):
    band, slab = lax.axis_index("band"), lax.axis_index("slab")
    core, column = lax.rem(slab, 2), lax.div(slab, 2)
    z, x_hi = lax.rem(column, 8), lax.div(column, 8)
    y, x = lax.div(band, 2), x_hi * 2 + lax.rem(band, 2)
    home, slot, half = lax.div(band, 4), lax.rem(band, 4), lax.div(z, 4)
    me = (x_hi * 8 + band) * 2 + core
    lower = core == 0
    at = lambda b, s: {"band": b, "slab": s}

    def layer(step, to_core):
        return at(band, (x_hi * 8 + lax.rem(z + step + 8, 8)) * 2 + to_core)

    load = pltpu.make_async_copy(tables, wt, table_sem)
    load.start()

    barrier = pltpu.get_barrier_semaphore()

    def greet_layer(k, _):
        j = lax.rem(me + k, PEERS)
        b, c = lax.rem(lax.div(j, 2), 8), lax.rem(j, 2)
        pl.semaphore_signal(barrier, inc=1, device_id=at(b, (lax.div(j, 16) * 8 + z) * 2 + c), device_id_type=MESH)
        return 0

    def greet_pillar(k, _):
        pl.semaphore_signal(barrier, inc=1, device_id=layer(lax.div(k, 2), lax.rem(k, 2)), device_id_type=MESH)
        return 0

    lax.fori_loop(1, PEERS, greet_layer, 0)
    lax.fori_loop(2, 16, greet_pillar, 0)
    pl.semaphore_wait(barrier, PEERS - 1 + 14)

    turned = [lax.rem(slot + i, 4) for i in range(4)]
    rank = lax.rem(band - z + 8, 8)
    in_held = sum(jnp.where(rank == e, 1, 0) for e in HELD)
    collector = 1 - in_held
    stays = jnp.logical_and(home == core, collector == core)

    def by_rank(visit):
        for r in range(8):
            pl.when(rank == r)(lambda r=r: visit(r))

    def gather(i):
        return pltpu.make_async_remote_copy(
            own.at[pl.ds(turned[i] * N, N)], vis.at[0, rank], gather_send.at[i], vis_recv.at[0, rank],
            device_id=at(4 * core + turned[i], column * 2 + collector), device_id_type=MESH)

    for i in range(1, 4):
        gather(i).start()
    keep = pltpu.make_async_copy(own.at[pl.ds(slot * N, N)], vis.at[0, rank], vis_recv.at[0, rank])
    pl.when(stays)(lambda: keep.start())
    pl.when(jnp.logical_not(stays))(lambda: gather(0).start())

    fold = lambda v: jnp.where(v < N // 2, v, v - N).astype(F32)
    line = lambda dim: lax.broadcasted_iota(jnp.int32, (N, N), dim)
    plane_sq = fold(line(0)) ** 2 + fold(line(1)) ** 2
    scale = N**1.5 / 4.0 / float(N) ** 3

    def coulomb(row):
        ky = fold(jnp.zeros((N, N), jnp.int32) + row)
        squared = plane_sq + ky * ky
        return jnp.where(squared > 0, scale / jnp.maximum(squared, 1.0), 0.0)

    for j in range(4):
        kern[j] = coulomb((x_hi * 8 + band) * 8 + core * 4 + j)
    row = 2 * me + half
    special = jnp.zeros((N, N), jnp.int32) + row == 0
    plain, nyquist = coulomb(row), coulomb(N // 2)
    kern[4] = jnp.where(special, 0.5 * (plain + nyquist), plain)
    kern[5] = jnp.where(special, 0.5 * (plain - nyquist), 0.0)
    flipped = jnp.where(lax.rem(line(0) + line(1), N) == 0, 1.0, 0.0).astype(BF16)
    half_in[...] = jnp.zeros(half_in.shape, F32)

    def left(stage, value, rows=2 * N, depth=2 * N):
        hi, lo = halves(value)
        high, low = wt[2 * stage, :rows, :depth], wt[2 * stage + 1, :rows, :depth]
        return mm(high, hi) + mm(high, lo) + mm(low, hi)

    def right(value, stage):
        hi, lo = halves(value)
        return mm(hi, wt[2 * stage]) + mm(lo, wt[2 * stage]) + mm(hi, wt[2 * stage + 1])

    def distance(k, of_core):
        return k + of_core * (7 - 2 * k)

    def plane_index(of_x_hi, of_band, k, of_core):
        return of_x_hi * 64 + lax.rem(z - distance(k, of_core) + 8, 8) * 8 + of_band

    def chips(visit):
        tos = [(lax.div(t, 2), lax.rem(t, 2)) for t in (lax.rem(x + i, 4) for i in (2, 1, 3, 0))]

        def step(k, _):
            to_y = lax.rem(y + lax.rem(k * 2, 4) + lax.div(k, 2), 4) * 2
            for to_hi, to_lo in tos:
                visit(to_hi, to_y + to_lo)
            return 0
        lax.fori_loop(1, 4, step, 0)
        for to_hi, to_lo in tos[:3]:
            visit(to_hi, y * 2 + to_lo)

    used = pl.ds(0, USED)

    def send_plane(k):
        mine = plane_index(x_hi, band, k, core)

        def visit(to_x_hi, to_band, to_core):
            pltpu.make_async_remote_copy(
                send_f.at[k, (to_x_hi * 8 + to_band) * 2 + to_core, used], recv_f.at[mine, used], f_send, f_recv,
                device_id=at(to_band, (to_x_hi * 8 + z) * 2 + to_core), device_id_type=MESH).start()

        chips(lambda *chip: [visit(*chip, to_core) for to_core in range(2)])
        visit(x_hi, band, 1 - core)
        pltpu.make_async_copy(send_f.at[k, me, used], recv_f.at[mine, used], f_local.at[k]).start()

    def return_planes(*planes):
        def visit(to_x_hi, to_band):
            for to_core, k in planes:
                pltpu.make_async_remote_copy(
                    send_b.at[plane_index(to_x_hi, to_band, k, to_core), used], recv_b.at[k, me, used], b_send, b_recv.at[k],
                    device_id=at(to_band, (to_x_hi * 8 + z) * 2 + to_core), device_id_type=MESH).start()

        chips(visit)
        for to_core, k in planes:
            @pl.when(core == to_core)
            def _():
                pltpu.make_async_copy(send_b.at[plane_index(x_hi, band, k, to_core), used], recv_b.at[k, me, used],
                                      b_local.at[k]).start()

            @pl.when(core != to_core)
            def _():
                pltpu.make_async_remote_copy(
                    send_b.at[plane_index(x_hi, band, k, to_core), used], recv_b.at[k, me, used], b_send, b_recv.at[k],
                    device_id=at(band, column * 2 + to_core), device_id_type=MESH).start()

    def arrived(k, e):
        pltpu.make_async_copy(vis.at[k, e], vis.at[k, e], vis_recv.at[k, e]).wait()

    def pass_on(here, k, r):
        for end in starts_at(here, r):
            to_core, to_k = place(end, r)
            source, target = (r - here) % 8, (r - end) % 8
            pltpu.make_async_remote_copy(
                vis.at[k, source], vis.at[to_k, target], relay_send, vis_recv.at[to_k, target],
                device_id=layer(stride_of(here, end), to_core), device_id_type=MESH).start()

    def start_plane(of_core, k):
        if k == 0:
            for r in (0, 4, 3, 1) if of_core == 0 else (7, 5, 2, 6):
                arrived(0, r)
                pass_on(0, 0, r)
        here = distance(k, of_core)
        ranks = [(here + e) % 8 for e in HELD]
        if here:
            for r in sorted(ranks, key=lambda r: -len(starts_at(here, r))):
                arrived(k, (r - here) % 8)
                pass_on(here, k, r)

    def analyse(k):
        f0, f1, f3, f4 = [vis[k, e] for e in HELD]
        fields = [f0 * f0, f0 * f1, f1 * f3, f0 * f3, f0 * f4, jnp.zeros((N, N), F32)]
        spec = right(tall([wide(fields[2 * p:2 * p + 2]) for p in range(3)]), INV)
        stacked = [tall([spec[p * N:(p + 1) * N, :N], spec[p * N:(p + 1) * N, N:]]) for p in range(3)]
        full = left(Y_FWD, wide(stacked[:2]))
        for p in range(2):
            send_f[k, :, 8 * p:8 * p + 8, :] = full[:, p * N:(p + 1) * N].reshape(PEERS, 8, N)
        half_out[...] = left(HALF_FWD, stacked[2], rows=N)
        flat = send_f.reshape(4 * PEERS * PITCH, N)
        for i in range(2):
            flat[pl.ds(k * PEERS * PITCH + 16 + i, PEERS, stride=PITCH), :] = half_out[pl.ds(2 * i + half, PEERS, stride=4), :]

    for k in range(4):
        pl.when(lower)(lambda k=k: start_plane(0, k))
        pl.when(jnp.logical_not(lower))(lambda k=k: start_plane(1, k))
        if k == 0:
            load.wait()
        analyse(k)
        send_plane(k)

    flat_f, flat_b = recv_f.reshape(N * PITCH, N), send_b.reshape(N * PITCH, N)
    for k in range(4):
        mine = plane_index(x_hi, band, k, core)
        pltpu.make_async_copy(send_f.at[k, me, used], recv_f.at[mine, used], f_local.at[k]).wait()
    arrivals = recv_f.at[pl.ds(0, 4 * (PEERS - 1)), used]
    pltpu.make_async_copy(arrivals, arrivals, f_recv).wait()

    def strip(r):
        return flat_f[pl.ds(r, N, stride=PITCH), :]

    def store(r, value):
        flat_b[pl.ds(r, N, stride=PITCH), :] = value

    for p in range(2):
        spec = left(FWD, wide([tall([strip(8 * p + j), strip(8 * p + 4 + j)]) for j in range(4)]))
        table = wide([kern[j] for j in range(4)])
        field = left(INV, tall([spec[:N] * table, spec[N:] * table]))
        for j in range(4):
            store(8 * p + j, field[:N, j * N:(j + 1) * N])
            store(8 * p + 4 + j, field[N:, j * N:(j + 1) * N])
    real, imag = strip(16), strip(17)
    hi, lo = halves(tall([real, -imag]))
    spec = left(FWD, wide([tall([real, imag]), mm(hi, flipped) + mm(lo, flipped)]))
    field = left(INV, tall([spec[i * N:(i + 1) * N, :N] * kern[4] + spec[i * N:(i + 1) * N, N:] * kern[5] for i in range(2)]))
    store(16, field[:N])
    store(17, field[N:])
    return_planes((1, 3))
    for k in (3, 2, 1):
        return_planes((0, k), (1, k - 1))
    return_planes((0, 0))

    def synthesise(k):
        mine = plane_index(x_hi, band, k, core)
        pltpu.make_async_copy(send_b.at[mine, used], recv_b.at[k, me, used], b_local.at[k]).wait()
        block = recv_b.at[k, pl.ds(0, PEERS - 1), used]
        pltpu.make_async_copy(block, block, b_recv.at[k]).wait()
        full = left(Y_INV, wide([recv_b[k, :, 8 * p:8 * p + 8, :].reshape(2 * N, N) for p in range(2)]))
        flat = recv_b.reshape(4 * PEERS * PITCH, N)
        for i in range(2):
            half_in[pl.ds(2 * i + half, PEERS, stride=4), :] = flat[pl.ds(k * PEERS * PITCH + 16 + i, PEERS, stride=PITCH), :]
        spec = [full[:, :N], full[:, N:], left(HALF_INV, half_in[...], depth=N)]
        both = right(tall([wide([s[:N], s[N:]]) for s in spec]), FWD)
        fields = [both[(e // 2) * N:(e // 2 + 1) * N, (e % 2) * N:(e % 2 + 1) * N] for e in range(5)]
        f0, f1, f3, f4 = [vis[k, e] for e in HELD]
        part[k, 0] = fields[0] * f0 + fields[1] * f1 + fields[3] * f3 + fields[4] * f4
        part[k, 1] = fields[1] * f0 + fields[2] * f3
        part[k, 3] = fields[2] * f1 + fields[3] * f0
        part[k, 4] = fields[4] * f0

    def pass_sums(of_core, k):
        here = distance(k, of_core)
        ranks = [(here + e) % 8 for e in HELD]
        for r in sorted(ranks, key=lambda r: len(starts_at(here, r))):
            e = (r - here) % 8
            if starts_at(here, r):
                pltpu.make_async_copy(inner.at[k, e], inner.at[k, e], inner_recv.at[k, e]).wait()
                part[k, e] += inner[k, e]
            (back,) = [start for start, end in ROUTES[r] if end == here]
            step = stride_of(back, here)
            if back:
                to_core, to_k = place(back, r)
                index = (to_k, (r - back) % 8)
                pltpu.make_async_remote_copy(part.at[k, e], inner.at[index], sum_send, inner_recv.at[index],
                                             device_id=layer(-step, to_core), device_id_type=MESH).start()
            else:
                hand_in(k, e, r, -step, 0 if step > 0 else 1).start()

    def hand_in(k, e, r, step, side):
        to_z = lax.rem(z + step + 8, 8)
        return pltpu.make_async_remote_copy(
            part.at[k, e], arrive.at[side, slot], sum_send, arrive_recv.at[side, slot],
            device_id=at(lax.rem(to_z + r, 8), (x_hi * 8 + to_z) * 2 + home), device_id_type=MESH)

    for k in (3, 2, 1, 0):
        synthesise(k)
        if k:
            pl.when(lower)(lambda k=k: pass_sums(0, k))
        pl.when(jnp.logical_not(lower))(lambda k=k: pass_sums(1, k))

    @pl.when(lower)
    def _():
        for r in HELD:
            keeps = jnp.logical_and(home == 0, rank == r)
            local = pltpu.make_async_copy(part.at[0, r], arrive.at[2, slot], arrive_recv.at[2, slot])
            pl.when(keeps)(lambda: local.start())
            pl.when(jnp.logical_not(keeps))(lambda: hand_in(0, r, r, 0, 2).start())

    def total_up(r):
        for q in range(4):
            for side in sides(r):
                pltpu.make_async_copy(arrive.at[side, q], arrive.at[side, q], arrive_recv.at[side, q]).wait()
            out[q * N:(q + 1) * N] = -0.25 * sum(arrive[side, q] for side in sides(r))

    by_rank(total_up)

    for i in range(1, 4):
        gather(i).wait_send()
    pl.when(jnp.logical_not(stays))(lambda: gather(0).wait_send())
    for sem, source in ((f_send, recv_f), (b_send, send_b)):
        block = source.at[pl.ds(0, 4 * (PEERS - 1)), used]
        pltpu.make_async_copy(block, block, sem).wait()

    def left_by(sem, ref, count):
        block = ref.reshape(32 * N, N).at[pl.ds(0, count * N)]
        pltpu.make_async_copy(block, block, sem).wait()

    pl.when(lower)(lambda: left_by(relay_send, vis, 13))
    pl.when(jnp.logical_not(lower))(lambda: left_by(relay_send, vis, 15))
    kept = jnp.logical_and(jnp.logical_and(lower, home == 0), in_held == 1)
    pl.when(kept)(lambda: left_by(sum_send, part, 15))
    pl.when(jnp.logical_not(kept))(lambda: left_by(sum_send, part, 16))


def per_device(wavefunctions, tables):
    dma = pltpu.SemaphoreType.DMA
    planes = lambda *shape: pltpu.VMEM((*shape, N, N), F32)
    by_peer, by_plane = pltpu.VMEM((4, PEERS, PITCH, N), F32), pltpu.VMEM((N, PITCH, N), F32)
    field = pl.pallas_call(
        kernel,
        out_shape=jax.ShapeDtypeStruct((4 * N, N), F32),
        in_specs=[pl.BlockSpec(memory_space=pltpu.HBM)] * 2,
        out_specs=pl.BlockSpec(memory_space=pltpu.VMEM),
        scratch_shapes=[
            pltpu.VMEM(tables.shape, BF16), planes(4, 8), planes(6), planes(4, 8), planes(4, 8), planes(3, 4), planes(), planes(), by_peer, by_plane, by_plane, by_peer,
            dma, dma((4,)), dma((4, 8)), dma, dma, dma, dma((4,)), dma, dma((4,)), dma((4,)), dma, dma((4, 8)), dma((3, 4)),
        ],
        compiler_params=pltpu.CompilerParams(collective_id=0, has_side_effects=True, vmem_limit_bytes=48 << 20),
        name="exchange",
    )(*[pltpu.with_memory_space_constraint(value, pltpu.HBM) for value in (wavefunctions.reshape(4 * N, N), tables)])
    return field.reshape(1, 4, N, N)


def solution(mesh):
    tables = weight_tables()
    spec = P("band", "slab", None, None)
    run = jax.shard_map(per_device, mesh=mesh, in_specs=(spec, P()), out_specs=spec, check_vma=False)
    return lambda wavefunctions: run(wavefunctions, jnp.asarray(tables))
```

```python
import jax
import jax.numpy as jnp
import ml_dtypes
import numpy as np
from jax import lax
from jax.experimental import pallas as pl
from jax.experimental.pallas import tpu as pltpu
from jax.sharding import PartitionSpec as P

MESH = pl.DeviceIdType.MESH
N = 128
PEERS = 32
USED, PITCH = 18, 24
BF16, F32 = jnp.bfloat16, jnp.float32
ALL, FIRST, REST = (0, USED), (0, 8), (8, USED - 8)
FWD, INV, Y_FWD, Y_INV, HALF_FWD, HALF_INV = range(6)

HELD = (0, 1, 3, 4)
ROUTES = (
    ((0, 7), (7, 5), (5, 4)),
    ((0, 1), (0, 6), (6, 5)),
    ((0, 1), (1, 2), (0, 7), (7, 6)),
    ((0, 2), (2, 3), (0, 7)),
    ((0, 1), (1, 3), (3, 4)),
    ((0, 1), (1, 2), (0, 5), (5, 4)),
    ((0, 2), (2, 3), (0, 6), (6, 5)),
    ((0, 3), (3, 4), (0, 7), (7, 6)),
)


def stride_of(start, end):
    return end - start if start <= end <= 4 and start < 4 else end - (start or 8)


def source_core(r):
    return 0 if r in HELD else 1


def place(distance, r):
    if distance == 0:
        return source_core(r), 0
    return (0, distance) if distance < 4 else (1, 7 - distance)


def starts_at(distance, r):
    return [end for start, end in ROUTES[r] if start == distance]


def sides(r):
    strides = [stride_of(0, end) for end in starts_at(0, r)]
    return [side for side, present in enumerate((max(strides) > 0, min(strides) < 0, r in HELD)) if present]


def weight_tables():
    index = np.arange(N)
    angle = 2.0 * np.pi / N * (index[:, None] * index[None, :] % N)
    cos, sin = np.cos(angle), np.sin(angle)
    forward = np.block([[cos, sin], [-sin, cos]])
    sign = 1.0 - 2.0 * (index % 2)
    ones = np.ones(N)

    def order(width):
        peer, part, sub = np.meshgrid(np.arange(PEERS), np.arange(2), np.arange(width), indexing="ij")
        return (part * N + peer * width + sub).reshape(-1)

    half_forward = forward.copy()
    half_forward[0] = np.concatenate([ones, -sign])
    half_forward[N] = np.concatenate([sign, ones])
    half_inverse = 2.0 * forward.T
    half_inverse[:, 0] = np.concatenate([ones, -sign])
    half_inverse[:, N] = np.concatenate([sign, ones])
    pad = np.zeros((2 * N, 2 * N))
    half_fwd, half_inv = pad.copy(), pad.copy()
    half_fwd[:N] = half_forward[order(2)]
    half_inv[:, :N] = half_inverse[:, order(2)]
    y_fwd = forward[order(4)]
    tables = []
    for stage in (forward, forward.T, y_fwd, y_fwd.T, half_fwd, half_inv):
        high = stage.astype(ml_dtypes.bfloat16)
        tables += [high, (stage - high.astype(np.float64)).astype(ml_dtypes.bfloat16)]
    return np.stack(tables)


def halves(value):
    high = value.astype(BF16)
    return high, (value - high.astype(F32)).astype(BF16)


def mm(a, b):
    return jnp.dot(a, b, preferred_element_type=F32)


def wide(values):
    return jnp.concatenate(values, axis=1)


def tall(values):
    return jnp.concatenate(values, axis=0)


def kernel(own, tables, out, wt, vis, kern, part, inner, arrive, half_out, half_in, send_f, recv_f, send_b, recv_b,
           table_sem, gather_send, vis_recv, relay_send, f_send, f_recv, f_local, b_send, b_recv, b_local, sum_send, inner_recv,
           arrive_recv, ready):
    band, slab = lax.axis_index("band"), lax.axis_index("slab")
    core, column = lax.rem(slab, 2), lax.div(slab, 2)
    z, x_hi = lax.rem(column, 8), lax.div(column, 8)
    y, x = lax.div(band, 2), x_hi * 2 + lax.rem(band, 2)
    home, slot, half = lax.div(band, 4), lax.rem(band, 4), lax.div(z, 4)
    me = (x_hi * 8 + band) * 2 + core
    lower = core == 0
    at = lambda b, s: {"band": b, "slab": s}

    def layer(step, to_core):
        return at(band, (x_hi * 8 + lax.rem(z + step + 8, 8)) * 2 + to_core)

    load = pltpu.make_async_copy(tables, wt, table_sem)
    load.start()

    barrier = pltpu.get_barrier_semaphore()

    def greet_group(semaphore):
        def greet(k, _):
            j = lax.rem(band * 2 + core + k, 16)
            pl.semaphore_signal(semaphore, inc=1, device_id=at(lax.div(j, 2), column * 2 + lax.rem(j, 2)), device_id_type=MESH)
            return 0
        lax.fori_loop(1, 16, greet, 0)

    def greet_pillar(k, _):
        pl.semaphore_signal(barrier, inc=1, device_id=layer(lax.div(k, 2), lax.rem(k, 2)), device_id_type=MESH)
        return 0

    greet_group(barrier)
    lax.fori_loop(2, 16, greet_pillar, 0)
    pl.semaphore_signal(barrier, inc=1, device_id=at(band, ((1 - x_hi) * 8 + z) * 2 + core), device_id_type=MESH)
    pl.semaphore_wait(barrier, 15 + 14 + 1)

    turned = [lax.rem(slot + i, 4) for i in range(4)]
    rank = lax.rem(band - z + 8, 8)
    in_held = sum(jnp.where(rank == e, 1, 0) for e in HELD)
    collector = 1 - in_held
    stays = jnp.logical_and(home == core, collector == core)

    def by_rank(visit):
        for r in range(8):
            pl.when(rank == r)(lambda r=r: visit(r))

    def gather(i):
        return pltpu.make_async_remote_copy(
            own.at[pl.ds(turned[i] * N, N)], vis.at[0, rank], gather_send.at[i], vis_recv.at[0, rank],
            device_id=at(4 * core + turned[i], column * 2 + collector), device_id_type=MESH)

    for i in range(1, 4):
        gather(i).start()
    keep = pltpu.make_async_copy(own.at[pl.ds(slot * N, N)], vis.at[0, rank], vis_recv.at[0, rank])
    pl.when(stays)(lambda: keep.start())
    pl.when(jnp.logical_not(stays))(lambda: gather(0).start())

    greet_group(ready)

    fold = lambda v: jnp.where(v < N // 2, v, v - N).astype(F32)
    line = lambda dim: lax.broadcasted_iota(jnp.int32, (N, N), dim)
    plane_sq = fold(line(0)) ** 2 + fold(line(1)) ** 2
    scale = N**1.5 / 4.0 / float(N) ** 3

    def coulomb(row):
        ky = fold(jnp.zeros((N, N), jnp.int32) + row)
        squared = plane_sq + ky * ky
        return jnp.where(squared > 0, scale / jnp.maximum(squared, 1.0), 0.0)

    for j in range(4):
        kern[j] = coulomb((x_hi * 8 + band) * 8 + core * 4 + j)
    row = 2 * me + half
    special = jnp.zeros((N, N), jnp.int32) + row == 0
    plain, nyquist = coulomb(row), coulomb(N // 2)
    kern[4] = jnp.where(special, 0.5 * (plain + nyquist), plain)
    kern[5] = jnp.where(special, 0.5 * (plain - nyquist), 0.0)
    flipped = jnp.where(lax.rem(line(0) + line(1), N) == 0, 1.0, 0.0).astype(BF16)
    half_in[...] = jnp.zeros(half_in.shape, F32)

    def left(stage, value, rows=2 * N, depth=2 * N):
        hi, lo = halves(value)
        high, low = wt[2 * stage, :rows, :depth], wt[2 * stage + 1, :rows, :depth]
        return mm(high, hi) + mm(high, lo) + mm(low, hi)

    def right(value, stage):
        hi, lo = halves(value)
        return mm(hi, wt[2 * stage]) + mm(lo, wt[2 * stage]) + mm(hi, wt[2 * stage + 1])

    def distance(k, of_core):
        return k + of_core * (7 - 2 * k)

    def plane_index(of_x_hi, of_band, k, of_core):
        return of_x_hi * 64 + lax.rem(z - distance(k, of_core) + 8, 8) * 8 + of_band

    def chips(visit):
        tos = [(lax.div(t, 2), lax.rem(t, 2)) for t in (lax.rem(x + i, 4) for i in (2, 1, 3, 0))]

        def step(k, _):
            to_y = lax.rem(y + lax.rem(k * 2, 4) + lax.div(k, 2), 4) * 2
            for to_hi, to_lo in tos:
                visit(to_hi, to_y + to_lo)
            return 0
        lax.fori_loop(1, 4, step, 0)
        for to_hi, to_lo in tos[:3]:
            visit(to_hi, y * 2 + to_lo)

    used = pl.ds(0, USED)

    def own_rows(k, rows, sem):
        mine, rows = plane_index(x_hi, band, k, core), pl.ds(*rows)
        return pltpu.make_async_copy(send_f.at[k, me, rows], recv_f.at[mine, rows], f_local.at[k + sem // 2])

    def send_plane(k, rows, sem):
        mine = plane_index(x_hi, band, k, core)

        def visit(to_x_hi, to_band, to_core):
            pltpu.make_async_remote_copy(
                send_f.at[k, (to_x_hi * 8 + to_band) * 2 + to_core, pl.ds(*rows)], recv_f.at[mine, pl.ds(*rows)], f_send,
                f_recv.at[sem],
                device_id=at(to_band, (to_x_hi * 8 + z) * 2 + to_core), device_id_type=MESH).start()

        chips(lambda *chip: [visit(*chip, to_core) for to_core in range(2)])
        visit(x_hi, band, 1 - core)
        own_rows(k, rows, sem).start()

    def return_planes(*planes, rows=ALL):
        def visit(to_x_hi, to_band):
            for to_core, k in planes:
                pltpu.make_async_remote_copy(
                    send_b.at[plane_index(to_x_hi, to_band, k, to_core), pl.ds(*rows)], recv_b.at[k, me, pl.ds(*rows)], b_send, b_recv.at[k],
                    device_id=at(to_band, (to_x_hi * 8 + z) * 2 + to_core), device_id_type=MESH).start()

        chips(visit)
        for to_core, k in planes:
            @pl.when(core == to_core)
            def _():
                pltpu.make_async_copy(send_b.at[plane_index(x_hi, band, k, to_core), pl.ds(*rows)], recv_b.at[k, me, pl.ds(*rows)],
                                      b_local.at[k + (rows == REST)]).start()

            @pl.when(core != to_core)
            def _():
                pltpu.make_async_remote_copy(
                    send_b.at[plane_index(x_hi, band, k, to_core), pl.ds(*rows)], recv_b.at[k, me, pl.ds(*rows)], b_send, b_recv.at[k],
                    device_id=at(band, column * 2 + to_core), device_id_type=MESH).start()

    def arrived(k, e):
        pltpu.make_async_copy(vis.at[k, e], vis.at[k, e], vis_recv.at[k, e]).wait()

    def pass_on(here, k, r, ends=None):
        for end in starts_at(here, r) if ends is None else ends:
            to_core, to_k = place(end, r)
            source, target = (r - here) % 8, (r - end) % 8
            pltpu.make_async_remote_copy(
                vis.at[k, source], vis.at[to_k, target], relay_send, vis_recv.at[to_k, target],
                device_id=layer(stride_of(here, end), to_core), device_id_type=MESH).start()

    def start_plane(of_core, k):
        if k == 0:
            mine = (0, 4, 3, 1) if of_core == 0 else (7, 5, 2, 6)
            for r in mine:
                arrived(0, r)
                pass_on(0, 0, r, [end for end in starts_at(0, r) if end in (1, 7)])
            for r in mine:
                pass_on(0, 0, r, [end for end in starts_at(0, r) if end not in (1, 7)])
        here = distance(k, of_core)
        ranks = [(here + e) % 8 for e in HELD]
        if here:
            for r in sorted(ranks, key=lambda r: -len(starts_at(here, r))):
                arrived(k, (r - here) % 8)
                pass_on(here, k, r)

    def analyse(k):
        f0, f1, f3, f4 = [vis[k, e] for e in HELD]
        spec = right(wide([f0 * f0, f0 * f1]), INV)
        send_f[k, :, 0:8, :] = left(Y_FWD, tall([spec[:, :N], spec[:, N:]])).reshape(PEERS, 8, N)
        if k == 3:
            send_plane(k, FIRST, 1)
        spec = right(tall([wide([f1 * f3, f0 * f3]), wide([f0 * f4, jnp.zeros((N, N), F32)])]), INV)
        stacked = [tall([spec[p * N:(p + 1) * N, :N], spec[p * N:(p + 1) * N, N:]]) for p in range(2)]
        send_f[k, :, 8:16, :] = left(Y_FWD, stacked[0]).reshape(PEERS, 8, N)
        half_out[...] = left(HALF_FWD, stacked[1], rows=N)
        flat = send_f.reshape(4 * PEERS * PITCH, N)
        for i in range(2):
            flat[pl.ds(k * PEERS * PITCH + 16 + i, PEERS, stride=PITCH), :] = half_out[pl.ds(2 * i + half, PEERS, stride=4), :]

    for k in range(4):
        pl.when(lower)(lambda k=k: start_plane(0, k))
        pl.when(jnp.logical_not(lower))(lambda k=k: start_plane(1, k))
        if k == 0:
            load.wait()
            pl.semaphore_wait(ready, 15)
        analyse(k)
        send_plane(k, REST if k == 3 else ALL, 2 if k == 3 else 0)

    flat_f, flat_b = recv_f.reshape(N * PITCH, N), send_b.reshape(N * PITCH, N)
    def received(sem, planes, rows):
        block = recv_f.at[pl.ds(0, planes * (PEERS - 1)), pl.ds(*rows)]
        pltpu.make_async_copy(block, block, f_recv.at[sem]).wait()

    for k in range(3):
        own_rows(k, ALL, 0).wait()
    received(0, 3, ALL)
    own_rows(3, FIRST, 1).wait()
    received(1, 1, FIRST)

    def strip(r):
        return flat_f[pl.ds(r, N, stride=PITCH), :]

    def store(r, value):
        flat_b[pl.ds(r, N, stride=PITCH), :] = value

    for p in range(2):
        if p == 1:
            own_rows(3, REST, 2).wait()
            received(2, 1, REST)
        spec = left(FWD, wide([tall([strip(8 * p + j), strip(8 * p + 4 + j)]) for j in range(4)]))
        table = wide([kern[j] for j in range(4)])
        field = left(INV, tall([spec[:N] * table, spec[N:] * table]))
        for j in range(4):
            store(8 * p + j, field[:N, j * N:(j + 1) * N])
            store(8 * p + 4 + j, field[N:, j * N:(j + 1) * N])
        if p == 0:
            return_planes((1, 3), rows=FIRST)
    real, imag = strip(16), strip(17)
    hi, lo = halves(tall([real, -imag]))
    spec = left(FWD, wide([tall([real, imag]), mm(hi, flipped) + mm(lo, flipped)]))
    field = left(INV, tall([spec[i * N:(i + 1) * N, :N] * kern[4] + spec[i * N:(i + 1) * N, N:] * kern[5] for i in range(2)]))
    store(16, field[:N])
    store(17, field[N:])
    return_planes((1, 3), rows=REST)
    for k in (3, 2, 1):
        return_planes((0, k), (1, k - 1))
    return_planes((0, 0))

    def synthesise(k):
        mine = plane_index(x_hi, band, k, core)
        def mine_back(rows, sem):
            rows = pl.ds(*rows)
            return pltpu.make_async_copy(send_b.at[mine, rows], recv_b.at[k, me, rows], b_local.at[sem])

        if k == 3:
            @pl.when(lower)
            def _():
                mine_back(ALL, 3).wait()

            @pl.when(jnp.logical_not(lower))
            def _():
                mine_back(FIRST, 3).wait()
                mine_back(REST, 4).wait()
        else:
            mine_back(ALL, k).wait()
        block = recv_b.at[k, pl.ds(0, PEERS - 1), used]
        pltpu.make_async_copy(block, block, b_recv.at[k]).wait()
        full = left(Y_INV, wide([recv_b[k, :, 8 * p:8 * p + 8, :].reshape(2 * N, N) for p in range(2)]))
        flat = recv_b.reshape(4 * PEERS * PITCH, N)
        for i in range(2):
            half_in[pl.ds(2 * i + half, PEERS, stride=4), :] = flat[pl.ds(k * PEERS * PITCH + 16 + i, PEERS, stride=PITCH), :]
        spec = [full[:, :N], full[:, N:], left(HALF_INV, half_in[...], depth=N)]
        both = right(tall([wide([s[:N], s[N:]]) for s in spec]), FWD)
        fields = [both[(e // 2) * N:(e // 2 + 1) * N, (e % 2) * N:(e % 2 + 1) * N] for e in range(5)]
        f0, f1, f3, f4 = [vis[k, e] for e in HELD]
        part[k, 0] = fields[0] * f0 + fields[1] * f1 + fields[3] * f3 + fields[4] * f4
        part[k, 1] = fields[1] * f0 + fields[2] * f3
        part[k, 3] = fields[2] * f1 + fields[3] * f0
        part[k, 4] = fields[4] * f0

    def pass_sums(of_core, k):
        here = distance(k, of_core)
        ranks = [(here + e) % 8 for e in HELD]
        for r in sorted(ranks, key=lambda r: len(starts_at(here, r))):
            e = (r - here) % 8
            if starts_at(here, r):
                pltpu.make_async_copy(inner.at[k, e], inner.at[k, e], inner_recv.at[k, e]).wait()
                part[k, e] += inner[k, e]
            (back,) = [start for start, end in ROUTES[r] if end == here]
            step = stride_of(back, here)
            if back:
                to_core, to_k = place(back, r)
                index = (to_k, (r - back) % 8)
                pltpu.make_async_remote_copy(part.at[k, e], inner.at[index], sum_send, inner_recv.at[index],
                                             device_id=layer(-step, to_core), device_id_type=MESH).start()
            else:
                hand_in(k, e, r, -step, 0 if step > 0 else 1).start()

    def hand_in(k, e, r, step, side):
        to_z = lax.rem(z + step + 8, 8)
        return pltpu.make_async_remote_copy(
            part.at[k, e], arrive.at[side, slot], sum_send, arrive_recv.at[side, slot],
            device_id=at(lax.rem(to_z + r, 8), (x_hi * 8 + to_z) * 2 + home), device_id_type=MESH)

    for k in (3, 2, 1, 0):
        synthesise(k)
        if k:
            pl.when(lower)(lambda k=k: pass_sums(0, k))
        pl.when(jnp.logical_not(lower))(lambda k=k: pass_sums(1, k))

    @pl.when(lower)
    def _():
        for r in HELD:
            keeps = jnp.logical_and(home == 0, rank == r)
            local = pltpu.make_async_copy(part.at[0, r], arrive.at[2, slot], arrive_recv.at[2, slot])
            pl.when(keeps)(lambda: local.start())
            pl.when(jnp.logical_not(keeps))(lambda: hand_in(0, r, r, 0, 2).start())

    def total_up(r):
        for q in range(4):
            for side in sides(r):
                pltpu.make_async_copy(arrive.at[side, q], arrive.at[side, q], arrive_recv.at[side, q]).wait()
            out[q * N:(q + 1) * N] = -0.25 * sum(arrive[side, q] for side in sides(r))

    by_rank(total_up)

    for i in range(1, 4):
        gather(i).wait_send()
    pl.when(jnp.logical_not(stays))(lambda: gather(0).wait_send())
    for sem, source in ((f_send, recv_f), (b_send, send_b)):
        block = source.at[pl.ds(0, 4 * (PEERS - 1)), used]
        pltpu.make_async_copy(block, block, sem).wait()

    def left_by(sem, ref, count):
        block = ref.reshape(32 * N, N).at[pl.ds(0, count * N)]
        pltpu.make_async_copy(block, block, sem).wait()

    pl.when(lower)(lambda: left_by(relay_send, vis, 13))
    pl.when(jnp.logical_not(lower))(lambda: left_by(relay_send, vis, 15))
    kept = jnp.logical_and(jnp.logical_and(lower, home == 0), in_held == 1)
    pl.when(kept)(lambda: left_by(sum_send, part, 15))
    pl.when(jnp.logical_not(kept))(lambda: left_by(sum_send, part, 16))


def per_device(wavefunctions, tables):
    dma = pltpu.SemaphoreType.DMA
    planes = lambda *shape: pltpu.VMEM((*shape, N, N), F32)
    by_peer, by_plane = pltpu.VMEM((4, PEERS, PITCH, N), F32), pltpu.VMEM((N, PITCH, N), F32)
    field = pl.pallas_call(
        kernel,
        out_shape=jax.ShapeDtypeStruct((4 * N, N), F32),
        in_specs=[pl.BlockSpec(memory_space=pltpu.HBM)] * 2,
        out_specs=pl.BlockSpec(memory_space=pltpu.VMEM),
        scratch_shapes=[
            pltpu.VMEM(tables.shape, BF16), planes(4, 8), planes(6), planes(4, 8), planes(4, 8), planes(3, 4), planes(), planes(), by_peer, by_plane, by_plane, by_peer,
            dma, dma((4,)), dma((4, 8)), dma, dma, dma((3,)), dma((5,)), dma, dma((4,)), dma((5,)), dma, dma((4, 8)), dma((3, 4)),
            pltpu.SemaphoreType.REGULAR,
        ],
        compiler_params=pltpu.CompilerParams(collective_id=0, has_side_effects=True, vmem_limit_bytes=48 << 20),
        name="exchange",
    )(*[pltpu.with_memory_space_constraint(value, pltpu.HBM) for value in (wavefunctions.reshape(4 * N, N), tables)])
    return field.reshape(1, 4, N, N)


def solution(mesh):
    tables = weight_tables()
    spec = P("band", "slab", None, None)
    run = jax.shard_map(per_device, mesh=mesh, in_specs=(spec, P()), out_specs=spec, check_vma=False)
    return lambda wavefunctions: run(wavefunctions, jnp.asarray(tables))
```

```python
import jax
import jax.numpy as jnp
import ml_dtypes
import numpy as np
from jax import lax
from jax.experimental import pallas as pl
from jax.experimental.pallas import tpu as pltpu
from jax.sharding import PartitionSpec as P

MESH = pl.DeviceIdType.MESH
N = 128
PEERS = 32
USED, PITCH = 18, 24
BF16, F32 = jnp.bfloat16, jnp.float32
ALL, FIRST, REST = (0, USED), (0, 8), (8, USED - 8)
ORDER = [(2, 2), (1, 1), (3, 3), (2, 1), (3, 1), (1, 3), (2, 3), (1, 2), (3, 2), (1, 0), (0, 3), (3, 0), (0, 1), (2, 0), (0, 2)]
FWD, INV, Y_FWD, Y_INV, HALF_FWD, HALF_INV = range(6)

HELD = (0, 1, 3, 4)
ROUTES = (
    ((0, 7), (7, 5), (5, 4)),
    ((0, 1), (0, 6), (6, 5)),
    ((0, 1), (1, 2), (0, 7), (7, 6)),
    ((0, 2), (2, 3), (0, 7)),
    ((0, 1), (1, 3), (3, 4)),
    ((0, 1), (1, 2), (0, 5), (5, 4)),
    ((0, 2), (2, 3), (0, 6), (6, 5)),
    ((0, 3), (3, 4), (0, 7), (7, 6)),
)


def stride_of(start, end):
    return end - start if start <= end <= 4 and start < 4 else end - (start or 8)


def source_core(r):
    return 0 if r in HELD else 1


def place(distance, r):
    if distance == 0:
        return source_core(r), 0
    return (0, distance) if distance < 4 else (1, 7 - distance)


def starts_at(distance, r):
    return [end for start, end in ROUTES[r] if start == distance]


def sides(r):
    strides = [stride_of(0, end) for end in starts_at(0, r)]
    return [side for side, present in enumerate((max(strides) > 0, min(strides) < 0, r in HELD)) if present]


def weight_tables():
    index = np.arange(N)
    angle = 2.0 * np.pi / N * (index[:, None] * index[None, :] % N)
    cos, sin = np.cos(angle), np.sin(angle)
    forward = np.block([[cos, sin], [-sin, cos]])
    sign = 1.0 - 2.0 * (index % 2)
    ones = np.ones(N)

    def order(width):
        peer, part, sub = np.meshgrid(np.arange(PEERS), np.arange(2), np.arange(width), indexing="ij")
        return (part * N + peer * width + sub).reshape(-1)

    half_forward = forward.copy()
    half_forward[0] = np.concatenate([ones, -sign])
    half_forward[N] = np.concatenate([sign, ones])
    half_inverse = 2.0 * forward.T
    half_inverse[:, 0] = np.concatenate([ones, -sign])
    half_inverse[:, N] = np.concatenate([sign, ones])
    pad = np.zeros((2 * N, 2 * N))
    half_fwd, half_inv = pad.copy(), pad.copy()
    half_fwd[:N] = half_forward[order(2)]
    half_inv[:, :N] = half_inverse[:, order(2)]
    y_fwd = forward[order(4)]
    tables = []
    for stage in (forward, forward.T, y_fwd, y_fwd.T, half_fwd, half_inv):
        high = stage.astype(ml_dtypes.bfloat16)
        tables += [high, (stage - high.astype(np.float64)).astype(ml_dtypes.bfloat16)]
    return np.stack(tables)


def halves(value):
    high = value.astype(BF16)
    return high, (value - high.astype(F32)).astype(BF16)


def mm(a, b):
    return jnp.dot(a, b, preferred_element_type=F32)


def wide(values):
    return jnp.concatenate(values, axis=1)


def tall(values):
    return jnp.concatenate(values, axis=0)


def kernel(own, tables, out, wt, vis, kern, part, inner, arrive, half_out, half_in, send_f, recv_f, send_b, recv_b,
           table_sem, gather_send, vis_recv, relay_send, f_send, f_recv, f_local, b_send, b_recv, b_local, sum_send, inner_recv,
           arrive_recv, ready):
    band, slab = lax.axis_index("band"), lax.axis_index("slab")
    core, column = lax.rem(slab, 2), lax.div(slab, 2)
    z, x_hi = lax.rem(column, 8), lax.div(column, 8)
    y, x = lax.div(band, 2), x_hi * 2 + lax.rem(band, 2)
    home, slot, half = lax.div(band, 4), lax.rem(band, 4), lax.div(z, 4)
    me = (x_hi * 8 + band) * 2 + core
    lower = core == 0
    at = lambda b, s: {"band": b, "slab": s}

    def layer(step, to_core):
        return at(band, (x_hi * 8 + lax.rem(z + step + 8, 8)) * 2 + to_core)

    load = pltpu.make_async_copy(tables, wt, table_sem)
    load.start()

    barrier = pltpu.get_barrier_semaphore()

    def greet_group(semaphore):
        def greet(k, _):
            j = lax.rem(band * 2 + core + k, 16)
            pl.semaphore_signal(semaphore, inc=1, device_id=at(lax.div(j, 2), column * 2 + lax.rem(j, 2)), device_id_type=MESH)
            return 0
        lax.fori_loop(1, 16, greet, 0)

    def greet_pillar(k, _):
        pl.semaphore_signal(barrier, inc=1, device_id=layer(lax.div(k, 2), lax.rem(k, 2)), device_id_type=MESH)
        return 0

    greet_group(barrier)
    lax.fori_loop(2, 16, greet_pillar, 0)
    pl.semaphore_signal(barrier, inc=1, device_id=at(band, ((1 - x_hi) * 8 + z) * 2 + core), device_id_type=MESH)
    pl.semaphore_wait(barrier, 15 + 14 + 1)

    turned = [lax.rem(slot + i, 4) for i in range(4)]
    rank = lax.rem(band - z + 8, 8)
    in_held = sum(jnp.where(rank == e, 1, 0) for e in HELD)
    collector = 1 - in_held
    stays = jnp.logical_and(home == core, collector == core)

    def by_rank(visit):
        for r in range(8):
            pl.when(rank == r)(lambda r=r: visit(r))

    def gather(i):
        return pltpu.make_async_remote_copy(
            own.at[pl.ds(turned[i] * N, N)], vis.at[0, rank], gather_send.at[i], vis_recv.at[0, rank],
            device_id=at(4 * core + turned[i], column * 2 + collector), device_id_type=MESH)

    for i in range(1, 4):
        gather(i).start()
    keep = pltpu.make_async_copy(own.at[pl.ds(slot * N, N)], vis.at[0, rank], vis_recv.at[0, rank])
    pl.when(stays)(lambda: keep.start())
    pl.when(jnp.logical_not(stays))(lambda: gather(0).start())

    greet_group(ready)

    fold = lambda v: jnp.where(v < N // 2, v, v - N).astype(F32)
    line = lambda dim: lax.broadcasted_iota(jnp.int32, (N, N), dim)
    plane_sq = fold(line(0)) ** 2 + fold(line(1)) ** 2
    scale = N**1.5 / 4.0 / float(N) ** 3

    def coulomb(row):
        ky = fold(jnp.zeros((N, N), jnp.int32) + row)
        squared = plane_sq + ky * ky
        return jnp.where(squared > 0, scale / jnp.maximum(squared, 1.0), 0.0)

    for j in range(4):
        kern[j] = coulomb((x_hi * 8 + band) * 8 + core * 4 + j)
    row = 2 * me + half
    special = jnp.zeros((N, N), jnp.int32) + row == 0
    plain, nyquist = coulomb(row), coulomb(N // 2)
    kern[4] = jnp.where(special, 0.5 * (plain + nyquist), plain)
    kern[5] = jnp.where(special, 0.5 * (plain - nyquist), 0.0)
    flipped = jnp.where(lax.rem(line(0) + line(1), N) == 0, 1.0, 0.0).astype(BF16)
    half_in[...] = jnp.zeros(half_in.shape, F32)

    def left(stage, value, rows=2 * N, depth=2 * N):
        hi, lo = halves(value)
        high, low = wt[2 * stage, :rows, :depth], wt[2 * stage + 1, :rows, :depth]
        return mm(high, hi) + mm(high, lo) + mm(low, hi)

    def right(value, stage):
        hi, lo = halves(value)
        return mm(hi, wt[2 * stage]) + mm(lo, wt[2 * stage]) + mm(hi, wt[2 * stage + 1])

    def distance(k, of_core):
        return k + of_core * (7 - 2 * k)

    def plane_index(of_x_hi, of_band, k, of_core):
        return of_x_hi * 64 + lax.rem(z - distance(k, of_core) + 8, 8) * 8 + of_band

    def chips(visit):
        at_x = [(lax.div(t, 2), lax.rem(t, 2)) for t in (lax.rem(x + i, 4) for i in range(4))]
        at_y = [lax.rem(y + i, 4) * 2 for i in range(4)]
        for i, j in ORDER:
            to_hi, to_lo = at_x[i]
            visit(to_hi, at_y[j] + to_lo)

    used = pl.ds(0, USED)

    def own_rows(k, rows, sem):
        mine, rows = plane_index(x_hi, band, k, core), pl.ds(*rows)
        return pltpu.make_async_copy(send_f.at[k, me, rows], recv_f.at[mine, rows], f_local.at[k + sem // 2])

    def send_plane(k, rows, sem):
        mine = plane_index(x_hi, band, k, core)

        def visit(to_x_hi, to_band, to_core):
            pltpu.make_async_remote_copy(
                send_f.at[k, (to_x_hi * 8 + to_band) * 2 + to_core, pl.ds(*rows)], recv_f.at[mine, pl.ds(*rows)], f_send,
                f_recv.at[sem],
                device_id=at(to_band, (to_x_hi * 8 + z) * 2 + to_core), device_id_type=MESH).start()

        chips(lambda *chip: [visit(*chip, to_core) for to_core in range(2)])
        visit(x_hi, band, 1 - core)
        own_rows(k, rows, sem).start()

    def return_planes(*planes, rows=ALL):
        def visit(to_x_hi, to_band):
            for to_core, k in planes:
                pltpu.make_async_remote_copy(
                    send_b.at[plane_index(to_x_hi, to_band, k, to_core), pl.ds(*rows)], recv_b.at[k, me, pl.ds(*rows)], b_send, b_recv.at[k],
                    device_id=at(to_band, (to_x_hi * 8 + z) * 2 + to_core), device_id_type=MESH).start()

        chips(visit)
        for to_core, k in planes:
            @pl.when(core == to_core)
            def _():
                pltpu.make_async_copy(send_b.at[plane_index(x_hi, band, k, to_core), pl.ds(*rows)], recv_b.at[k, me, pl.ds(*rows)],
                                      b_local.at[k + (rows == REST)]).start()

            @pl.when(core != to_core)
            def _():
                pltpu.make_async_remote_copy(
                    send_b.at[plane_index(x_hi, band, k, to_core), pl.ds(*rows)], recv_b.at[k, me, pl.ds(*rows)], b_send, b_recv.at[k],
                    device_id=at(band, column * 2 + to_core), device_id_type=MESH).start()

    def arrived(k, e):
        pltpu.make_async_copy(vis.at[k, e], vis.at[k, e], vis_recv.at[k, e]).wait()

    def pass_on(here, k, r, ends=None):
        for end in starts_at(here, r) if ends is None else ends:
            to_core, to_k = place(end, r)
            source, target = (r - here) % 8, (r - end) % 8
            pltpu.make_async_remote_copy(
                vis.at[k, source], vis.at[to_k, target], relay_send, vis_recv.at[to_k, target],
                device_id=layer(stride_of(here, end), to_core), device_id_type=MESH).start()

    def start_plane(of_core, k):
        if k == 0:
            mine = (0, 4, 3, 1) if of_core == 0 else (7, 5, 2, 6)
            for r in mine:
                arrived(0, r)
                pass_on(0, 0, r, [end for end in starts_at(0, r) if end in (1, 7)])
            for r in mine:
                pass_on(0, 0, r, [end for end in starts_at(0, r) if end not in (1, 7)])
        here = distance(k, of_core)
        ranks = [(here + e) % 8 for e in HELD]
        if here:
            for r in sorted(ranks, key=lambda r: -len(starts_at(here, r))):
                arrived(k, (r - here) % 8)
                pass_on(here, k, r)

    def analyse(k):
        f0, f1, f3, f4 = [vis[k, e] for e in HELD]
        spec = right(wide([f0 * f0, f0 * f1]), INV)
        send_f[k, :, 0:8, :] = left(Y_FWD, tall([spec[:, :N], spec[:, N:]])).reshape(PEERS, 8, N)
        if k == 3:
            send_plane(k, FIRST, 1)
        spec = right(tall([wide([f1 * f3, f0 * f3]), wide([f0 * f4, jnp.zeros((N, N), F32)])]), INV)
        stacked = [tall([spec[p * N:(p + 1) * N, :N], spec[p * N:(p + 1) * N, N:]]) for p in range(2)]
        send_f[k, :, 8:16, :] = left(Y_FWD, stacked[0]).reshape(PEERS, 8, N)
        half_out[...] = left(HALF_FWD, stacked[1], rows=N)
        flat = send_f.reshape(4 * PEERS * PITCH, N)
        for i in range(2):
            flat[pl.ds(k * PEERS * PITCH + 16 + i, PEERS, stride=PITCH), :] = half_out[pl.ds(2 * i + half, PEERS, stride=4), :]

    for k in range(4):
        pl.when(lower)(lambda k=k: start_plane(0, k))
        pl.when(jnp.logical_not(lower))(lambda k=k: start_plane(1, k))
        if k == 0:
            load.wait()
            pl.semaphore_wait(ready, 15)
        analyse(k)
        send_plane(k, REST if k == 3 else ALL, 2 if k == 3 else 0)

    flat_f, flat_b = recv_f.reshape(N * PITCH, N), send_b.reshape(N * PITCH, N)
    def received(sem, planes, rows):
        block = recv_f.at[pl.ds(0, planes * (PEERS - 1)), pl.ds(*rows)]
        pltpu.make_async_copy(block, block, f_recv.at[sem]).wait()

    for k in range(3):
        own_rows(k, ALL, 0).wait()
    received(0, 3, ALL)
    own_rows(3, FIRST, 1).wait()
    received(1, 1, FIRST)

    def strip(r):
        return flat_f[pl.ds(r, N, stride=PITCH), :]

    def store(r, value):
        flat_b[pl.ds(r, N, stride=PITCH), :] = value

    for p in range(2):
        if p == 1:
            own_rows(3, REST, 2).wait()
            received(2, 1, REST)
        spec = left(FWD, wide([tall([strip(8 * p + j), strip(8 * p + 4 + j)]) for j in range(4)]))
        table = wide([kern[j] for j in range(4)])
        field = left(INV, tall([spec[:N] * table, spec[N:] * table]))
        for j in range(4):
            store(8 * p + j, field[:N, j * N:(j + 1) * N])
            store(8 * p + 4 + j, field[N:, j * N:(j + 1) * N])
        if p == 0:
            return_planes((1, 3), rows=FIRST)
    real, imag = strip(16), strip(17)
    hi, lo = halves(tall([real, -imag]))
    spec = left(FWD, wide([tall([real, imag]), mm(hi, flipped) + mm(lo, flipped)]))
    field = left(INV, tall([spec[i * N:(i + 1) * N, :N] * kern[4] + spec[i * N:(i + 1) * N, N:] * kern[5] for i in range(2)]))
    store(16, field[:N])
    store(17, field[N:])
    return_planes((1, 3), rows=REST)
    for k in (3, 2, 1):
        return_planes((0, k))
        return_planes((1, k - 1))
    return_planes((0, 0))

    def synthesise(k):
        mine = plane_index(x_hi, band, k, core)
        def mine_back(rows, sem):
            rows = pl.ds(*rows)
            return pltpu.make_async_copy(send_b.at[mine, rows], recv_b.at[k, me, rows], b_local.at[sem])

        if k == 3:
            @pl.when(lower)
            def _():
                mine_back(ALL, 3).wait()

            @pl.when(jnp.logical_not(lower))
            def _():
                mine_back(FIRST, 3).wait()
                mine_back(REST, 4).wait()
        else:
            mine_back(ALL, k).wait()
        block = recv_b.at[k, pl.ds(0, PEERS - 1), used]
        pltpu.make_async_copy(block, block, b_recv.at[k]).wait()
        full = left(Y_INV, wide([recv_b[k, :, 8 * p:8 * p + 8, :].reshape(2 * N, N) for p in range(2)]))
        flat = recv_b.reshape(4 * PEERS * PITCH, N)
        for i in range(2):
            half_in[pl.ds(2 * i + half, PEERS, stride=4), :] = flat[pl.ds(k * PEERS * PITCH + 16 + i, PEERS, stride=PITCH), :]
        spec = [full[:, :N], full[:, N:], left(HALF_INV, half_in[...], depth=N)]
        both = right(tall([wide([s[:N], s[N:]]) for s in spec]), FWD)
        fields = [both[(e // 2) * N:(e // 2 + 1) * N, (e % 2) * N:(e % 2 + 1) * N] for e in range(5)]
        f0, f1, f3, f4 = [vis[k, e] for e in HELD]
        part[k, 0] = fields[0] * f0 + fields[1] * f1 + fields[3] * f3 + fields[4] * f4
        part[k, 1] = fields[1] * f0 + fields[2] * f3
        part[k, 3] = fields[2] * f1 + fields[3] * f0
        part[k, 4] = fields[4] * f0

    def pass_sums(of_core, k):
        here = distance(k, of_core)
        ranks = [(here + e) % 8 for e in HELD]
        for r in sorted(ranks, key=lambda r: len(starts_at(here, r))):
            e = (r - here) % 8
            if starts_at(here, r):
                pltpu.make_async_copy(inner.at[k, e], inner.at[k, e], inner_recv.at[k, e]).wait()
                part[k, e] += inner[k, e]
            (back,) = [start for start, end in ROUTES[r] if end == here]
            step = stride_of(back, here)
            if back:
                to_core, to_k = place(back, r)
                index = (to_k, (r - back) % 8)
                pltpu.make_async_remote_copy(part.at[k, e], inner.at[index], sum_send, inner_recv.at[index],
                                             device_id=layer(-step, to_core), device_id_type=MESH).start()
            else:
                hand_in(k, e, r, -step, 0 if step > 0 else 1).start()

    def hand_in(k, e, r, step, side):
        to_z = lax.rem(z + step + 8, 8)
        return pltpu.make_async_remote_copy(
            part.at[k, e], arrive.at[side, slot], sum_send, arrive_recv.at[side, slot],
            device_id=at(lax.rem(to_z + r, 8), (x_hi * 8 + to_z) * 2 + home), device_id_type=MESH)

    for k in (3, 2, 1, 0):
        synthesise(k)
        if k:
            pl.when(lower)(lambda k=k: pass_sums(0, k))
        pl.when(jnp.logical_not(lower))(lambda k=k: pass_sums(1, k))

    @pl.when(lower)
    def _():
        for r in HELD:
            keeps = jnp.logical_and(home == 0, rank == r)
            local = pltpu.make_async_copy(part.at[0, r], arrive.at[2, slot], arrive_recv.at[2, slot])
            pl.when(keeps)(lambda: local.start())
            pl.when(jnp.logical_not(keeps))(lambda: hand_in(0, r, r, 0, 2).start())

    def total_up(r):
        for q in range(4):
            for side in sides(r):
                pltpu.make_async_copy(arrive.at[side, q], arrive.at[side, q], arrive_recv.at[side, q]).wait()
            out[q * N:(q + 1) * N] = -0.25 * sum(arrive[side, q] for side in sides(r))

    by_rank(total_up)

    for i in range(1, 4):
        gather(i).wait_send()
    pl.when(jnp.logical_not(stays))(lambda: gather(0).wait_send())
    for sem, source in ((f_send, recv_f), (b_send, send_b)):
        block = source.at[pl.ds(0, 4 * (PEERS - 1)), used]
        pltpu.make_async_copy(block, block, sem).wait()

    def left_by(sem, ref, count):
        block = ref.reshape(32 * N, N).at[pl.ds(0, count * N)]
        pltpu.make_async_copy(block, block, sem).wait()

    pl.when(lower)(lambda: left_by(relay_send, vis, 13))
    pl.when(jnp.logical_not(lower))(lambda: left_by(relay_send, vis, 15))
    kept = jnp.logical_and(jnp.logical_and(lower, home == 0), in_held == 1)
    pl.when(kept)(lambda: left_by(sum_send, part, 15))
    pl.when(jnp.logical_not(kept))(lambda: left_by(sum_send, part, 16))


def per_device(wavefunctions, tables):
    dma = pltpu.SemaphoreType.DMA
    planes = lambda *shape: pltpu.VMEM((*shape, N, N), F32)
    by_peer, by_plane = pltpu.VMEM((4, PEERS, PITCH, N), F32), pltpu.VMEM((N, PITCH, N), F32)
    field = pl.pallas_call(
        kernel,
        out_shape=jax.ShapeDtypeStruct((4 * N, N), F32),
        in_specs=[pl.BlockSpec(memory_space=pltpu.HBM)] * 2,
        out_specs=pl.BlockSpec(memory_space=pltpu.VMEM),
        scratch_shapes=[
            pltpu.VMEM(tables.shape, BF16), planes(4, 8), planes(6), planes(4, 8), planes(4, 8), planes(3, 4), planes(), planes(), by_peer, by_plane, by_plane, by_peer,
            dma, dma((4,)), dma((4, 8)), dma, dma, dma((3,)), dma((5,)), dma, dma((4,)), dma((5,)), dma, dma((4, 8)), dma((3, 4)),
            pltpu.SemaphoreType.REGULAR,
        ],
        compiler_params=pltpu.CompilerParams(collective_id=0, has_side_effects=True, vmem_limit_bytes=48 << 20),
        name="exchange",
    )(*[pltpu.with_memory_space_constraint(value, pltpu.HBM) for value in (wavefunctions.reshape(4 * N, N), tables)])
    return field.reshape(1, 4, N, N)


def solution(mesh):
    tables = weight_tables()
    spec = P("band", "slab", None, None)
    run = jax.shard_map(per_device, mesh=mesh, in_specs=(spec, P()), out_specs=spec, check_vma=False)
    return lambda wavefunctions: run(wavefunctions, jnp.asarray(tables))
```

```python
import jax
import jax.numpy as jnp
import ml_dtypes
import numpy as np
from jax import lax
from jax.experimental import pallas as pl
from jax.experimental.pallas import tpu as pltpu
from jax.sharding import PartitionSpec as P

MESH = pl.DeviceIdType.MESH
N = 128
PEERS = 32
USED, PITCH = 18, 24
BF16, F32 = jnp.bfloat16, jnp.float32
COLLECTED = ((2, 3), (6, 1))
ALL, FIRST, REST = (0, USED), (0, 8), (8, USED - 8)
ORDER = [(2, 2), (1, 1), (3, 3), (2, 1), (3, 1), (1, 3), (2, 3), (1, 2), (3, 2), (1, 0), (0, 3), (3, 0), (0, 1), (2, 0), (0, 2)]
FWD, INV, Y_FWD, Y_INV, HALF_FWD, HALF_INV = range(6)

HELD = (0, 1, 3, 4)
ROUTES = (
    ((0, 7), (7, 5), (5, 4)),
    ((0, 1), (0, 6), (6, 5)),
    ((0, 1), (1, 2), (0, 7), (7, 6)),
    ((0, 2), (2, 3), (0, 7)),
    ((0, 1), (1, 3), (3, 4)),
    ((0, 1), (1, 2), (0, 5), (5, 4)),
    ((0, 2), (2, 3), (0, 6), (6, 5)),
    ((0, 3), (3, 4), (0, 7), (7, 6)),
)


def stride_of(start, end):
    return end - start if start <= end <= 4 and start < 4 else end - (start or 8)


def source_core(r):
    return 0 if r in HELD else 1


def place(distance, r):
    if distance == 0:
        return source_core(r), 0
    return (0, distance) if distance < 4 else (1, 7 - distance)


def starts_at(distance, r):
    return [end for start, end in ROUTES[r] if start == distance]


def sides(r):
    strides = [stride_of(0, end) for end in starts_at(0, r) if (end, r) not in COLLECTED]
    return [side for side, present in enumerate((max(strides) > 0, min(strides) < 0, r in HELD)) if present]


def weight_tables():
    index = np.arange(N)
    angle = 2.0 * np.pi / N * (index[:, None] * index[None, :] % N)
    cos, sin = np.cos(angle), np.sin(angle)
    forward = np.block([[cos, sin], [-sin, cos]])
    sign = 1.0 - 2.0 * (index % 2)
    ones = np.ones(N)

    def order(width):
        peer, part, sub = np.meshgrid(np.arange(PEERS), np.arange(2), np.arange(width), indexing="ij")
        return (part * N + peer * width + sub).reshape(-1)

    half_forward = forward.copy()
    half_forward[0] = np.concatenate([ones, -sign])
    half_forward[N] = np.concatenate([sign, ones])
    half_inverse = 2.0 * forward.T
    half_inverse[:, 0] = np.concatenate([ones, -sign])
    half_inverse[:, N] = np.concatenate([sign, ones])
    pad = np.zeros((2 * N, 2 * N))
    half_fwd, half_inv = pad.copy(), pad.copy()
    half_fwd[:N] = half_forward[order(2)]
    half_inv[:, :N] = half_inverse[:, order(2)]
    y_fwd = forward[order(4)]
    tables = []
    for stage in (forward, forward.T, y_fwd, y_fwd.T, half_fwd, half_inv):
        high = stage.astype(ml_dtypes.bfloat16)
        tables += [high, (stage - high.astype(np.float64)).astype(ml_dtypes.bfloat16)]
    return np.stack(tables)


def halves(value):
    high = value.astype(BF16)
    return high, (value - high.astype(F32)).astype(BF16)


def mm(a, b):
    return jnp.dot(a, b, preferred_element_type=F32)


def wide(values):
    return jnp.concatenate(values, axis=1)


def tall(values):
    return jnp.concatenate(values, axis=0)


def kernel(own, tables, out, wt, vis, kern, part, inner, arrive, half_out, half_in, send_f, recv_f, send_b, recv_b,
           table_sem, gather_send, vis_recv, relay_send, f_send, f_recv, f_local, b_send, b_recv, b_local, sum_send, inner_recv,
           arrive_recv, ready):
    band, slab = lax.axis_index("band"), lax.axis_index("slab")
    core, column = lax.rem(slab, 2), lax.div(slab, 2)
    z, x_hi = lax.rem(column, 8), lax.div(column, 8)
    y, x = lax.div(band, 2), x_hi * 2 + lax.rem(band, 2)
    home, slot, half = lax.div(band, 4), lax.rem(band, 4), lax.div(z, 4)
    me = (x_hi * 8 + band) * 2 + core
    lower = core == 0
    at = lambda b, s: {"band": b, "slab": s}

    def layer(step, to_core):
        return at(band, (x_hi * 8 + lax.rem(z + step + 8, 8)) * 2 + to_core)

    load = pltpu.make_async_copy(tables, wt, table_sem)
    load.start()

    barrier = pltpu.get_barrier_semaphore()

    def greet_group(semaphore):
        def greet(k, _):
            j = lax.rem(band * 2 + core + k, 16)
            pl.semaphore_signal(semaphore, inc=1, device_id=at(lax.div(j, 2), column * 2 + lax.rem(j, 2)), device_id_type=MESH)
            return 0
        lax.fori_loop(1, 16, greet, 0)

    def greet_pillar(k, _):
        pl.semaphore_signal(barrier, inc=1, device_id=layer(lax.div(k, 2), lax.rem(k, 2)), device_id_type=MESH)
        return 0

    greet_group(barrier)
    lax.fori_loop(2, 16, greet_pillar, 0)
    pl.semaphore_signal(barrier, inc=1, device_id=at(band, ((1 - x_hi) * 8 + z) * 2 + core), device_id_type=MESH)
    pl.semaphore_wait(barrier, 15 + 14 + 1)

    turned = [lax.rem(slot + i, 4) for i in range(4)]
    rank = lax.rem(band - z + 8, 8)
    in_held = sum(jnp.where(rank == e, 1, 0) for e in HELD)
    collector = 1 - in_held
    stays = jnp.logical_and(home == core, collector == core)

    def by_rank(visit):
        for r in range(8):
            pl.when(rank == r)(lambda r=r: visit(r))

    def gather(i):
        return pltpu.make_async_remote_copy(
            own.at[pl.ds(turned[i] * N, N)], vis.at[0, rank], gather_send.at[i], vis_recv.at[0, rank],
            device_id=at(4 * core + turned[i], column * 2 + collector), device_id_type=MESH)

    for i in range(1, 4):
        gather(i).start()
    keep = pltpu.make_async_copy(own.at[pl.ds(slot * N, N)], vis.at[0, rank], vis_recv.at[0, rank])
    pl.when(stays)(lambda: keep.start())
    pl.when(jnp.logical_not(stays))(lambda: gather(0).start())

    greet_group(ready)

    fold = lambda v: jnp.where(v < N // 2, v, v - N).astype(F32)
    line = lambda dim: lax.broadcasted_iota(jnp.int32, (N, N), dim)
    plane_sq = fold(line(0)) ** 2 + fold(line(1)) ** 2
    scale = N**1.5 / 4.0 / float(N) ** 3

    def coulomb(row):
        ky = fold(jnp.zeros((N, N), jnp.int32) + row)
        squared = plane_sq + ky * ky
        return jnp.where(squared > 0, scale / jnp.maximum(squared, 1.0), 0.0)

    for j in range(4):
        kern[j] = coulomb((x_hi * 8 + band) * 8 + core * 4 + j)
    row = 2 * me + half
    special = jnp.zeros((N, N), jnp.int32) + row == 0
    plain, nyquist = coulomb(row), coulomb(N // 2)
    kern[4] = jnp.where(special, 0.5 * (plain + nyquist), plain)
    kern[5] = jnp.where(special, 0.5 * (plain - nyquist), 0.0)
    flipped = jnp.where(lax.rem(line(0) + line(1), N) == 0, 1.0, 0.0).astype(BF16)
    half_in[...] = jnp.zeros(half_in.shape, F32)

    def left(stage, value, rows=2 * N, depth=2 * N):
        hi, lo = halves(value)
        high, low = wt[2 * stage, :rows, :depth], wt[2 * stage + 1, :rows, :depth]
        return mm(high, hi) + mm(high, lo) + mm(low, hi)

    def right(value, stage):
        hi, lo = halves(value)
        return mm(hi, wt[2 * stage]) + mm(lo, wt[2 * stage]) + mm(hi, wt[2 * stage + 1])

    def distance(k, of_core):
        return k + of_core * (7 - 2 * k)

    def plane_index(of_x_hi, of_band, k, of_core):
        return of_x_hi * 64 + lax.rem(z - distance(k, of_core) + 8, 8) * 8 + of_band

    def chips(visit):
        at_x = [(lax.div(t, 2), lax.rem(t, 2)) for t in (lax.rem(x + i, 4) for i in range(4))]
        at_y = [lax.rem(y + i, 4) * 2 for i in range(4)]
        for i, j in ORDER:
            to_hi, to_lo = at_x[i]
            visit(to_hi, at_y[j] + to_lo)

    used = pl.ds(0, USED)

    def own_rows(k, rows, sem):
        mine, rows = plane_index(x_hi, band, k, core), pl.ds(*rows)
        return pltpu.make_async_copy(send_f.at[k, me, rows], recv_f.at[mine, rows], f_local.at[k + sem // 2])

    def send_plane(k, rows, sem):
        mine = plane_index(x_hi, band, k, core)

        def visit(to_x_hi, to_band, to_core):
            pltpu.make_async_remote_copy(
                send_f.at[k, (to_x_hi * 8 + to_band) * 2 + to_core, pl.ds(*rows)], recv_f.at[mine, pl.ds(*rows)], f_send,
                f_recv.at[sem],
                device_id=at(to_band, (to_x_hi * 8 + z) * 2 + to_core), device_id_type=MESH).start()

        chips(lambda *chip: [visit(*chip, to_core) for to_core in range(2)])
        visit(x_hi, band, 1 - core)
        own_rows(k, rows, sem).start()

    def return_planes(*planes, rows=ALL):
        def visit(to_x_hi, to_band):
            for to_core, k in planes:
                pltpu.make_async_remote_copy(
                    send_b.at[plane_index(to_x_hi, to_band, k, to_core), pl.ds(*rows)], recv_b.at[k, me, pl.ds(*rows)], b_send, b_recv.at[k],
                    device_id=at(to_band, (to_x_hi * 8 + z) * 2 + to_core), device_id_type=MESH).start()

        chips(visit)
        for to_core, k in planes:
            @pl.when(core == to_core)
            def _():
                pltpu.make_async_copy(send_b.at[plane_index(x_hi, band, k, to_core), pl.ds(*rows)], recv_b.at[k, me, pl.ds(*rows)],
                                      b_local.at[k + (rows == REST)]).start()

            @pl.when(core != to_core)
            def _():
                pltpu.make_async_remote_copy(
                    send_b.at[plane_index(x_hi, band, k, to_core), pl.ds(*rows)], recv_b.at[k, me, pl.ds(*rows)], b_send, b_recv.at[k],
                    device_id=at(band, column * 2 + to_core), device_id_type=MESH).start()

    def arrived(k, e):
        pltpu.make_async_copy(vis.at[k, e], vis.at[k, e], vis_recv.at[k, e]).wait()

    def pass_on(here, k, r, ends=None):
        for end in starts_at(here, r) if ends is None else ends:
            to_core, to_k = place(end, r)
            source, target = (r - here) % 8, (r - end) % 8
            pltpu.make_async_remote_copy(
                vis.at[k, source], vis.at[to_k, target], relay_send, vis_recv.at[to_k, target],
                device_id=layer(stride_of(here, end), to_core), device_id_type=MESH).start()

    def start_plane(of_core, k):
        if k == 0:
            mine = (0, 4, 3, 1) if of_core == 0 else (7, 5, 2, 6)
            for r in mine:
                arrived(0, r)
                pass_on(0, 0, r, [end for end in starts_at(0, r) if end in (1, 7)])
            for r in mine:
                pass_on(0, 0, r, [end for end in starts_at(0, r) if end not in (1, 7)])
        here = distance(k, of_core)
        ranks = [(here + e) % 8 for e in HELD]
        if here:
            for r in sorted(ranks, key=lambda r: -len(starts_at(here, r))):
                arrived(k, (r - here) % 8)
                pass_on(here, k, r)

    def analyse(k):
        f0, f1, f3, f4 = [vis[k, e] for e in HELD]
        spec = right(wide([f0 * f0, f0 * f1]), INV)
        send_f[k, :, 0:8, :] = left(Y_FWD, tall([spec[:, :N], spec[:, N:]])).reshape(PEERS, 8, N)
        if k == 3:
            send_plane(k, FIRST, 1)
        spec = right(tall([wide([f1 * f3, f0 * f3]), wide([f0 * f4, jnp.zeros((N, N), F32)])]), INV)
        stacked = [tall([spec[p * N:(p + 1) * N, :N], spec[p * N:(p + 1) * N, N:]]) for p in range(2)]
        send_f[k, :, 8:16, :] = left(Y_FWD, stacked[0]).reshape(PEERS, 8, N)
        half_out[...] = left(HALF_FWD, stacked[1], rows=N)
        flat = send_f.reshape(4 * PEERS * PITCH, N)
        for i in range(2):
            flat[pl.ds(k * PEERS * PITCH + 16 + i, PEERS, stride=PITCH), :] = half_out[pl.ds(2 * i + half, PEERS, stride=4), :]

    for k in range(4):
        pl.when(lower)(lambda k=k: start_plane(0, k))
        pl.when(jnp.logical_not(lower))(lambda k=k: start_plane(1, k))
        if k == 0:
            load.wait()
            pl.semaphore_wait(ready, 15)
        analyse(k)
        send_plane(k, REST if k == 3 else ALL, 2 if k == 3 else 0)

    flat_f, flat_b = recv_f.reshape(N * PITCH, N), send_b.reshape(N * PITCH, N)
    def received(sem, planes, rows):
        block = recv_f.at[pl.ds(0, planes * (PEERS - 1)), pl.ds(*rows)]
        pltpu.make_async_copy(block, block, f_recv.at[sem]).wait()

    for k in range(3):
        own_rows(k, ALL, 0).wait()
    received(0, 3, ALL)
    own_rows(3, FIRST, 1).wait()
    received(1, 1, FIRST)

    def strip(r):
        return flat_f[pl.ds(r, N, stride=PITCH), :]

    def store(r, value):
        flat_b[pl.ds(r, N, stride=PITCH), :] = value

    for p in range(2):
        if p == 1:
            own_rows(3, REST, 2).wait()
            received(2, 1, REST)
        spec = left(FWD, wide([tall([strip(8 * p + j), strip(8 * p + 4 + j)]) for j in range(4)]))
        table = wide([kern[j] for j in range(4)])
        field = left(INV, tall([spec[:N] * table, spec[N:] * table]))
        for j in range(4):
            store(8 * p + j, field[:N, j * N:(j + 1) * N])
            store(8 * p + 4 + j, field[N:, j * N:(j + 1) * N])
        if p == 0:
            return_planes((1, 3), (0, 3), rows=FIRST)
    real, imag = strip(16), strip(17)
    hi, lo = halves(tall([real, -imag]))
    spec = left(FWD, wide([tall([real, imag]), mm(hi, flipped) + mm(lo, flipped)]))
    field = left(INV, tall([spec[i * N:(i + 1) * N, :N] * kern[4] + spec[i * N:(i + 1) * N, N:] * kern[5] for i in range(2)]))
    store(16, field[:N])
    store(17, field[N:])
    return_planes((1, 3), (0, 3), rows=REST)
    for k in (2, 1, 0):
        return_planes((1, k))
        return_planes((0, k))

    def synthesise(k):
        mine = plane_index(x_hi, band, k, core)
        def mine_back(rows, sem):
            rows = pl.ds(*rows)
            return pltpu.make_async_copy(send_b.at[mine, rows], recv_b.at[k, me, rows], b_local.at[sem])

        if k == 3:
            mine_back(FIRST, 3).wait()
            mine_back(REST, 4).wait()
        else:
            mine_back(ALL, k).wait()
        block = recv_b.at[k, pl.ds(0, PEERS - 1), used]
        pltpu.make_async_copy(block, block, b_recv.at[k]).wait()
        full = left(Y_INV, wide([recv_b[k, :, 8 * p:8 * p + 8, :].reshape(2 * N, N) for p in range(2)]))
        flat = recv_b.reshape(4 * PEERS * PITCH, N)
        for i in range(2):
            half_in[pl.ds(2 * i + half, PEERS, stride=4), :] = flat[pl.ds(k * PEERS * PITCH + 16 + i, PEERS, stride=PITCH), :]
        spec = [full[:, :N], full[:, N:], left(HALF_INV, half_in[...], depth=N)]
        both = right(tall([wide([s[:N], s[N:]]) for s in spec]), FWD)
        fields = [both[(e // 2) * N:(e // 2 + 1) * N, (e % 2) * N:(e % 2 + 1) * N] for e in range(5)]
        f0, f1, f3, f4 = [vis[k, e] for e in HELD]
        part[k, 0] = fields[0] * f0 + fields[1] * f1 + fields[3] * f3 + fields[4] * f4
        part[k, 1] = fields[1] * f0 + fields[2] * f3
        part[k, 3] = fields[2] * f1 + fields[3] * f0
        part[k, 4] = fields[4] * f0

    def pass_sums(of_core, k):
        here = distance(k, of_core)
        ranks = [(here + e) % 8 for e in HELD]
        for r in sorted(ranks, key=lambda r: len(starts_at(here, r))):
            e = (r - here) % 8
            if starts_at(here, r):
                pltpu.make_async_copy(inner.at[k, e], inner.at[k, e], inner_recv.at[k, e]).wait()
                part[k, e] += inner[k, e]
            (back,) = [start for start, end in ROUTES[r] if end == here]
            step = stride_of(back, here)
            if back:
                to_core, to_k = place(back, r)
                index = (to_k, (r - back) % 8)
                pltpu.make_async_remote_copy(part.at[k, e], inner.at[index], sum_send, inner_recv.at[index],
                                             device_id=layer(-step, to_core), device_id_type=MESH).start()
            elif (here, r) in COLLECTED:
                pltpu.make_async_remote_copy(part.at[k, e], inner.at[0, r], sum_send, inner_recv.at[0, r],
                                             device_id=layer(-step, 0), device_id_type=MESH).start()
            else:
                hand_in(k, e, r, -step, 0 if step > 0 else 1).start()

    def hand_in(k, e, r, step, side):
        to_z = lax.rem(z + step + 8, 8)
        return pltpu.make_async_remote_copy(
            part.at[k, e], arrive.at[side, slot], sum_send, arrive_recv.at[side, slot],
            device_id=at(lax.rem(to_z + r, 8), (x_hi * 8 + to_z) * 2 + home), device_id_type=MESH)

    for k in (3, 2, 1, 0):
        synthesise(k)
        if k:
            pl.when(lower)(lambda k=k: pass_sums(0, k))
        pl.when(jnp.logical_not(lower))(lambda k=k: pass_sums(1, k))

    @pl.when(lower)
    def _():
        for r in HELD:
            if any(r == collected for _, collected in COLLECTED):
                pltpu.make_async_copy(inner.at[0, r], inner.at[0, r], inner_recv.at[0, r]).wait()
                part[0, r] += inner[0, r]
            keeps = jnp.logical_and(home == 0, rank == r)
            local = pltpu.make_async_copy(part.at[0, r], arrive.at[2, slot], arrive_recv.at[2, slot])
            pl.when(keeps)(lambda: local.start())
            pl.when(jnp.logical_not(keeps))(lambda: hand_in(0, r, r, 0, 2).start())

    def total_up(r):
        for q in range(4):
            for side in sides(r):
                pltpu.make_async_copy(arrive.at[side, q], arrive.at[side, q], arrive_recv.at[side, q]).wait()
            out[q * N:(q + 1) * N] = -0.25 * sum(arrive[side, q] for side in sides(r))

    by_rank(total_up)

    for i in range(1, 4):
        gather(i).wait_send()
    pl.when(jnp.logical_not(stays))(lambda: gather(0).wait_send())
    for sem, source in ((f_send, recv_f), (b_send, send_b)):
        block = source.at[pl.ds(0, 4 * (PEERS - 1)), used]
        pltpu.make_async_copy(block, block, sem).wait()

    def left_by(sem, ref, count):
        block = ref.reshape(32 * N, N).at[pl.ds(0, count * N)]
        pltpu.make_async_copy(block, block, sem).wait()

    pl.when(lower)(lambda: left_by(relay_send, vis, 13))
    pl.when(jnp.logical_not(lower))(lambda: left_by(relay_send, vis, 15))
    kept = jnp.logical_and(jnp.logical_and(lower, home == 0), in_held == 1)
    pl.when(kept)(lambda: left_by(sum_send, part, 15))
    pl.when(jnp.logical_not(kept))(lambda: left_by(sum_send, part, 16))


def per_device(wavefunctions, tables):
    dma = pltpu.SemaphoreType.DMA
    planes = lambda *shape: pltpu.VMEM((*shape, N, N), F32)
    by_peer, by_plane = pltpu.VMEM((4, PEERS, PITCH, N), F32), pltpu.VMEM((N, PITCH, N), F32)
    field = pl.pallas_call(
        kernel,
        out_shape=jax.ShapeDtypeStruct((4 * N, N), F32),
        in_specs=[pl.BlockSpec(memory_space=pltpu.HBM)] * 2,
        out_specs=pl.BlockSpec(memory_space=pltpu.VMEM),
        scratch_shapes=[
            pltpu.VMEM(tables.shape, BF16), planes(4, 8), planes(6), planes(4, 8), planes(4, 8), planes(3, 4), planes(), planes(), by_peer, by_plane, by_plane, by_peer,
            dma, dma((4,)), dma((4, 8)), dma, dma, dma((3,)), dma((5,)), dma, dma((4,)), dma((5,)), dma, dma((4, 8)), dma((3, 4)),
            pltpu.SemaphoreType.REGULAR,
        ],
        compiler_params=pltpu.CompilerParams(collective_id=0, has_side_effects=True, vmem_limit_bytes=48 << 20),
        name="exchange",
    )(*[pltpu.with_memory_space_constraint(value, pltpu.HBM) for value in (wavefunctions.reshape(4 * N, N), tables)])
    return field.reshape(1, 4, N, N)


def solution(mesh):
    tables = weight_tables()
    spec = P("band", "slab", None, None)
    run = jax.shard_map(per_device, mesh=mesh, in_specs=(spec, P()), out_specs=spec, check_vma=False)
    return lambda wavefunctions: run(wavefunctions, jnp.asarray(tables))
```

```python
import jax
import jax.numpy as jnp
import ml_dtypes
import numpy as np
from jax import lax
from jax.experimental import pallas as pl
from jax.experimental.pallas import tpu as pltpu
from jax.sharding import PartitionSpec as P

MESH = pl.DeviceIdType.MESH
N = 128
PEERS = 32
USED, PITCH = 18, 24
BF16, F32 = jnp.bfloat16, jnp.float32
COLLECTED = ((2, 3), (6, 1), (2, 6), (6, 6))
ALL, FIRST, REST = (0, USED), (0, 8), (8, USED - 8)
ORDER = [(2, 2), (1, 1), (3, 3), (2, 1), (3, 1), (1, 3), (2, 3), (1, 2), (3, 2), (1, 0), (0, 3), (3, 0), (0, 1), (2, 0), (0, 2)]
FWD, INV, Y_FWD, Y_INV, HALF_FWD, HALF_INV = range(6)

HELD = (0, 1, 3, 4)
ROUTES = (
    ((0, 7), (7, 5), (5, 4)),
    ((0, 1), (0, 6), (6, 5)),
    ((0, 1), (1, 2), (0, 7), (7, 6)),
    ((0, 2), (2, 3), (0, 7)),
    ((0, 1), (1, 3), (3, 4)),
    ((0, 1), (1, 2), (0, 5), (5, 4)),
    ((0, 2), (2, 3), (0, 6), (6, 5)),
    ((0, 3), (3, 4), (0, 7), (7, 6)),
)


def stride_of(start, end):
    return end - start if start <= end <= 4 and start < 4 else end - (start or 8)


def source_core(r):
    return 0 if r in HELD else 1


def place(distance, r):
    if distance == 0:
        return source_core(r), 0
    return (0, distance) if distance < 4 else (1, 7 - distance)


def starts_at(distance, r):
    return [end for start, end in ROUTES[r] if start == distance]


def sides(r):
    if r == 6:
        return [0]
    strides = [stride_of(0, end) for end in starts_at(0, r) if (end, r) not in COLLECTED]
    return [side for side, present in enumerate((max(strides) > 0, min(strides) < 0, r in HELD)) if present]


def weight_tables():
    index = np.arange(N)
    angle = 2.0 * np.pi / N * (index[:, None] * index[None, :] % N)
    cos, sin = np.cos(angle), np.sin(angle)
    forward = np.block([[cos, sin], [-sin, cos]])
    sign = 1.0 - 2.0 * (index % 2)
    ones = np.ones(N)

    def order(width):
        peer, part, sub = np.meshgrid(np.arange(PEERS), np.arange(2), np.arange(width), indexing="ij")
        return (part * N + peer * width + sub).reshape(-1)

    half_forward = forward.copy()
    half_forward[0] = np.concatenate([ones, -sign])
    half_forward[N] = np.concatenate([sign, ones])
    half_inverse = 2.0 * forward.T
    half_inverse[:, 0] = np.concatenate([ones, -sign])
    half_inverse[:, N] = np.concatenate([sign, ones])
    pad = np.zeros((2 * N, 2 * N))
    half_fwd, half_inv = pad.copy(), pad.copy()
    half_fwd[:N] = half_forward[order(2)]
    half_inv[:, :N] = half_inverse[:, order(2)]
    y_fwd = forward[order(4)]
    tables = []
    for stage in (forward, forward.T, y_fwd, y_fwd.T, half_fwd, half_inv):
        high = stage.astype(ml_dtypes.bfloat16)
        tables += [high, (stage - high.astype(np.float64)).astype(ml_dtypes.bfloat16)]
    return np.stack(tables)


def halves(value):
    high = value.astype(BF16)
    return high, (value - high.astype(F32)).astype(BF16)


def mm(a, b):
    return jnp.dot(a, b, preferred_element_type=F32)


def wide(values):
    return jnp.concatenate(values, axis=1)


def tall(values):
    return jnp.concatenate(values, axis=0)


def kernel(own, tables, out, wt, vis, kern, part, inner, arrive, half_out, half_in, send_f, recv_f, send_b, recv_b,
           table_sem, gather_send, vis_recv, relay_send, f_send, f_recv, f_local, b_send, b_recv, b_local, sum_send, inner_recv,
           arrive_recv, ready):
    band, slab = lax.axis_index("band"), lax.axis_index("slab")
    core, column = lax.rem(slab, 2), lax.div(slab, 2)
    z, x_hi = lax.rem(column, 8), lax.div(column, 8)
    y, x = lax.div(band, 2), x_hi * 2 + lax.rem(band, 2)
    home, slot, half = lax.div(band, 4), lax.rem(band, 4), lax.div(z, 4)
    me = (x_hi * 8 + band) * 2 + core
    lower = core == 0
    at = lambda b, s: {"band": b, "slab": s}

    def layer(step, to_core):
        return at(band, (x_hi * 8 + lax.rem(z + step + 8, 8)) * 2 + to_core)

    load = pltpu.make_async_copy(tables, wt, table_sem)
    load.start()

    barrier = pltpu.get_barrier_semaphore()

    def greet_group(semaphore):
        def greet(k, _):
            j = lax.rem(band * 2 + core + k, 16)
            pl.semaphore_signal(semaphore, inc=1, device_id=at(lax.div(j, 2), column * 2 + lax.rem(j, 2)), device_id_type=MESH)
            return 0
        lax.fori_loop(1, 16, greet, 0)

    def greet_pillar(k, _):
        pl.semaphore_signal(barrier, inc=1, device_id=layer(lax.div(k, 2), lax.rem(k, 2)), device_id_type=MESH)
        return 0

    greet_group(barrier)
    lax.fori_loop(2, 16, greet_pillar, 0)
    pl.semaphore_signal(barrier, inc=1, device_id=at(band, ((1 - x_hi) * 8 + z) * 2 + core), device_id_type=MESH)
    pl.semaphore_wait(barrier, 15 + 14 + 1)

    turned = [lax.rem(slot + i, 4) for i in range(4)]
    rank = lax.rem(band - z + 8, 8)
    in_held = sum(jnp.where(rank == e, 1, 0) for e in HELD)
    collector = 1 - in_held
    stays = jnp.logical_and(home == core, collector == core)

    def by_rank(visit):
        for r in range(8):
            pl.when(rank == r)(lambda r=r: visit(r))

    def gather(i):
        return pltpu.make_async_remote_copy(
            own.at[pl.ds(turned[i] * N, N)], vis.at[0, rank], gather_send.at[i], vis_recv.at[0, rank],
            device_id=at(4 * core + turned[i], column * 2 + collector), device_id_type=MESH)

    for i in range(1, 4):
        gather(i).start()
    keep = pltpu.make_async_copy(own.at[pl.ds(slot * N, N)], vis.at[0, rank], vis_recv.at[0, rank])
    pl.when(stays)(lambda: keep.start())
    pl.when(jnp.logical_not(stays))(lambda: gather(0).start())

    greet_group(ready)

    fold = lambda v: jnp.where(v < N // 2, v, v - N).astype(F32)
    line = lambda dim: lax.broadcasted_iota(jnp.int32, (N, N), dim)
    plane_sq = fold(line(0)) ** 2 + fold(line(1)) ** 2
    scale = N**1.5 / 4.0 / float(N) ** 3

    def coulomb(row):
        ky = fold(jnp.zeros((N, N), jnp.int32) + row)
        squared = plane_sq + ky * ky
        return jnp.where(squared > 0, scale / jnp.maximum(squared, 1.0), 0.0)

    for j in range(4):
        kern[j] = coulomb((x_hi * 8 + band) * 8 + core * 4 + j)
    row = 2 * me + half
    special = jnp.zeros((N, N), jnp.int32) + row == 0
    plain, nyquist = coulomb(row), coulomb(N // 2)
    kern[4] = jnp.where(special, 0.5 * (plain + nyquist), plain)
    kern[5] = jnp.where(special, 0.5 * (plain - nyquist), 0.0)
    flipped = jnp.where(lax.rem(line(0) + line(1), N) == 0, 1.0, 0.0).astype(BF16)
    half_in[...] = jnp.zeros(half_in.shape, F32)

    def left(stage, value, rows=2 * N, depth=2 * N):
        hi, lo = halves(value)
        high, low = wt[2 * stage, :rows, :depth], wt[2 * stage + 1, :rows, :depth]
        return mm(high, hi) + mm(high, lo) + mm(low, hi)

    def right(value, stage):
        hi, lo = halves(value)
        return mm(hi, wt[2 * stage]) + mm(lo, wt[2 * stage]) + mm(hi, wt[2 * stage + 1])

    def distance(k, of_core):
        return k + of_core * (7 - 2 * k)

    def plane_index(of_x_hi, of_band, k, of_core):
        return of_x_hi * 64 + lax.rem(z - distance(k, of_core) + 8, 8) * 8 + of_band

    def chips(visit):
        at_x = [(lax.div(t, 2), lax.rem(t, 2)) for t in (lax.rem(x + i, 4) for i in range(4))]
        at_y = [lax.rem(y + i, 4) * 2 for i in range(4)]
        for i, j in ORDER:
            to_hi, to_lo = at_x[i]
            visit(to_hi, at_y[j] + to_lo)

    used = pl.ds(0, USED)

    def own_rows(k, rows, sem):
        mine, rows = plane_index(x_hi, band, k, core), pl.ds(*rows)
        return pltpu.make_async_copy(send_f.at[k, me, rows], recv_f.at[mine, rows], f_local.at[k + sem // 2])

    def send_plane(k, rows, sem):
        mine = plane_index(x_hi, band, k, core)

        def visit(to_x_hi, to_band, to_core):
            pltpu.make_async_remote_copy(
                send_f.at[k, (to_x_hi * 8 + to_band) * 2 + to_core, pl.ds(*rows)], recv_f.at[mine, pl.ds(*rows)], f_send,
                f_recv.at[sem],
                device_id=at(to_band, (to_x_hi * 8 + z) * 2 + to_core), device_id_type=MESH).start()

        chips(lambda *chip: [visit(*chip, to_core) for to_core in range(2)])
        visit(x_hi, band, 1 - core)
        own_rows(k, rows, sem).start()

    def return_planes(*planes, rows=ALL):
        def visit(to_x_hi, to_band):
            for to_core, k in planes:
                pltpu.make_async_remote_copy(
                    send_b.at[plane_index(to_x_hi, to_band, k, to_core), pl.ds(*rows)], recv_b.at[k, me, pl.ds(*rows)], b_send, b_recv.at[k],
                    device_id=at(to_band, (to_x_hi * 8 + z) * 2 + to_core), device_id_type=MESH).start()

        chips(visit)
        for to_core, k in planes:
            @pl.when(core == to_core)
            def _():
                pltpu.make_async_copy(send_b.at[plane_index(x_hi, band, k, to_core), pl.ds(*rows)], recv_b.at[k, me, pl.ds(*rows)],
                                      b_local.at[k + (rows == REST)]).start()

            @pl.when(core != to_core)
            def _():
                pltpu.make_async_remote_copy(
                    send_b.at[plane_index(x_hi, band, k, to_core), pl.ds(*rows)], recv_b.at[k, me, pl.ds(*rows)], b_send, b_recv.at[k],
                    device_id=at(band, column * 2 + to_core), device_id_type=MESH).start()

    def arrived(k, e):
        pltpu.make_async_copy(vis.at[k, e], vis.at[k, e], vis_recv.at[k, e]).wait()

    def pass_on(here, k, r, ends=None):
        for end in starts_at(here, r) if ends is None else ends:
            to_core, to_k = place(end, r)
            source, target = (r - here) % 8, (r - end) % 8
            pltpu.make_async_remote_copy(
                vis.at[k, source], vis.at[to_k, target], relay_send, vis_recv.at[to_k, target],
                device_id=layer(stride_of(here, end), to_core), device_id_type=MESH).start()

    def start_plane(of_core, k):
        if k == 0:
            mine = (0, 4, 3, 1) if of_core == 0 else (7, 5, 2, 6)
            for r in mine:
                arrived(0, r)
                pass_on(0, 0, r, [end for end in starts_at(0, r) if end in (1, 7)])
            for r in mine:
                pass_on(0, 0, r, [end for end in starts_at(0, r) if end not in (1, 7)])
        here = distance(k, of_core)
        ranks = [(here + e) % 8 for e in HELD]
        if here:
            for r in sorted(ranks, key=lambda r: -len(starts_at(here, r))):
                arrived(k, (r - here) % 8)
                pass_on(here, k, r)

    def analyse(k):
        f0, f1, f3, f4 = [vis[k, e] for e in HELD]
        spec = right(wide([f0 * f0, f0 * f1]), INV)
        send_f[k, :, 0:8, :] = left(Y_FWD, tall([spec[:, :N], spec[:, N:]])).reshape(PEERS, 8, N)
        if k == 3:
            send_plane(k, FIRST, 1)
        spec = right(tall([wide([f1 * f3, f0 * f3]), wide([f0 * f4, jnp.zeros((N, N), F32)])]), INV)
        stacked = [tall([spec[p * N:(p + 1) * N, :N], spec[p * N:(p + 1) * N, N:]]) for p in range(2)]
        send_f[k, :, 8:16, :] = left(Y_FWD, stacked[0]).reshape(PEERS, 8, N)
        half_out[...] = left(HALF_FWD, stacked[1], rows=N)
        flat = send_f.reshape(4 * PEERS * PITCH, N)
        for i in range(2):
            flat[pl.ds(k * PEERS * PITCH + 16 + i, PEERS, stride=PITCH), :] = half_out[pl.ds(2 * i + half, PEERS, stride=4), :]

    for k in range(4):
        pl.when(lower)(lambda k=k: start_plane(0, k))
        pl.when(jnp.logical_not(lower))(lambda k=k: start_plane(1, k))
        if k == 0:
            load.wait()
            pl.semaphore_wait(ready, 15)
        analyse(k)
        send_plane(k, REST if k == 3 else ALL, 2 if k == 3 else 0)

    flat_f, flat_b = recv_f.reshape(N * PITCH, N), send_b.reshape(N * PITCH, N)
    def received(sem, planes, rows):
        block = recv_f.at[pl.ds(0, planes * (PEERS - 1)), pl.ds(*rows)]
        pltpu.make_async_copy(block, block, f_recv.at[sem]).wait()

    for k in range(3):
        own_rows(k, ALL, 0).wait()
    received(0, 3, ALL)
    own_rows(3, FIRST, 1).wait()
    received(1, 1, FIRST)

    def strip(r):
        return flat_f[pl.ds(r, N, stride=PITCH), :]

    def store(r, value):
        flat_b[pl.ds(r, N, stride=PITCH), :] = value

    for p in range(2):
        if p == 1:
            own_rows(3, REST, 2).wait()
            received(2, 1, REST)
        spec = left(FWD, wide([tall([strip(8 * p + j), strip(8 * p + 4 + j)]) for j in range(4)]))
        table = wide([kern[j] for j in range(4)])
        field = left(INV, tall([spec[:N] * table, spec[N:] * table]))
        for j in range(4):
            store(8 * p + j, field[:N, j * N:(j + 1) * N])
            store(8 * p + 4 + j, field[N:, j * N:(j + 1) * N])
        if p == 0:
            return_planes((1, 3), (0, 3), rows=FIRST)
    real, imag = strip(16), strip(17)
    hi, lo = halves(tall([real, -imag]))
    spec = left(FWD, wide([tall([real, imag]), mm(hi, flipped) + mm(lo, flipped)]))
    field = left(INV, tall([spec[i * N:(i + 1) * N, :N] * kern[4] + spec[i * N:(i + 1) * N, N:] * kern[5] for i in range(2)]))
    store(16, field[:N])
    store(17, field[N:])
    return_planes((1, 3), (0, 3), rows=REST)
    for k in (2, 1, 0):
        return_planes((1, k))
        return_planes((0, k))

    def synthesise(k):
        mine = plane_index(x_hi, band, k, core)
        def mine_back(rows, sem):
            rows = pl.ds(*rows)
            return pltpu.make_async_copy(send_b.at[mine, rows], recv_b.at[k, me, rows], b_local.at[sem])

        if k == 3:
            mine_back(FIRST, 3).wait()
            mine_back(REST, 4).wait()
        else:
            mine_back(ALL, k).wait()
        block = recv_b.at[k, pl.ds(0, PEERS - 1), used]
        pltpu.make_async_copy(block, block, b_recv.at[k]).wait()
        full = left(Y_INV, wide([recv_b[k, :, 8 * p:8 * p + 8, :].reshape(2 * N, N) for p in range(2)]))
        flat = recv_b.reshape(4 * PEERS * PITCH, N)
        for i in range(2):
            half_in[pl.ds(2 * i + half, PEERS, stride=4), :] = flat[pl.ds(k * PEERS * PITCH + 16 + i, PEERS, stride=PITCH), :]
        spec = [full[:, :N], full[:, N:], left(HALF_INV, half_in[...], depth=N)]
        both = right(tall([wide([s[:N], s[N:]]) for s in spec]), FWD)
        fields = [both[(e // 2) * N:(e // 2 + 1) * N, (e % 2) * N:(e % 2 + 1) * N] for e in range(5)]
        f0, f1, f3, f4 = [vis[k, e] for e in HELD]
        part[k, 0] = fields[0] * f0 + fields[1] * f1 + fields[3] * f3 + fields[4] * f4
        part[k, 1] = fields[1] * f0 + fields[2] * f3
        part[k, 3] = fields[2] * f1 + fields[3] * f0
        part[k, 4] = fields[4] * f0

    def pass_sums(of_core, k):
        here = distance(k, of_core)
        ranks = [(here + e) % 8 for e in HELD]
        for r in sorted(ranks, key=lambda r: len(starts_at(here, r))):
            e = (r - here) % 8
            if starts_at(here, r):
                pltpu.make_async_copy(inner.at[k, e], inner.at[k, e], inner_recv.at[k, e]).wait()
                part[k, e] += inner[k, e]
            (back,) = [start for start, end in ROUTES[r] if end == here]
            step = stride_of(back, here)
            if back:
                to_core, to_k = place(back, r)
                index = (to_k, (r - back) % 8)
                pltpu.make_async_remote_copy(part.at[k, e], inner.at[index], sum_send, inner_recv.at[index],
                                             device_id=layer(-step, to_core), device_id_type=MESH).start()
            elif (here, r) in COLLECTED:
                index = (0, 7 if r == 6 and step < 0 else r)
                pltpu.make_async_remote_copy(part.at[k, e], inner.at[index], sum_send, inner_recv.at[index],
                                             device_id=layer(-step, source_core(r)), device_id_type=MESH).start()
            else:
                hand_in(k, e, r, -step, 0 if step > 0 else 1).start()

    def hand_in(k, e, r, step, side):
        to_z = lax.rem(z + step + 8, 8)
        return pltpu.make_async_remote_copy(
            part.at[k, e], arrive.at[side, slot], sum_send, arrive_recv.at[side, slot],
            device_id=at(lax.rem(to_z + r, 8), (x_hi * 8 + to_z) * 2 + home), device_id_type=MESH)

    kept_six = jnp.logical_and(home == 1, rank == 6)

    def join_sums():
        for e in (6, 7):
            pltpu.make_async_copy(inner.at[0, e], inner.at[0, e], inner_recv.at[0, e]).wait()
        part[0, 6] = inner[0, 6] + inner[0, 7]
        local = pltpu.make_async_copy(part.at[0, 6], arrive.at[0, slot], arrive_recv.at[0, slot])
        pl.when(kept_six)(lambda: local.start())
        pl.when(jnp.logical_not(kept_six))(lambda: hand_in(0, 6, 6, 0, 0).start())

    for k in (3, 2, 1, 0):
        synthesise(k)
        if k:
            pl.when(lower)(lambda k=k: pass_sums(0, k))
        pl.when(jnp.logical_not(lower))(lambda k=k: pass_sums(1, k))
        if k == 1:
            pl.when(jnp.logical_not(lower))(join_sums)

    @pl.when(lower)
    def _():
        for r in HELD:
            if any(r == collected for _, collected in COLLECTED):
                pltpu.make_async_copy(inner.at[0, r], inner.at[0, r], inner_recv.at[0, r]).wait()
                part[0, r] += inner[0, r]
            keeps = jnp.logical_and(home == 0, rank == r)
            local = pltpu.make_async_copy(part.at[0, r], arrive.at[2, slot], arrive_recv.at[2, slot])
            pl.when(keeps)(lambda: local.start())
            pl.when(jnp.logical_not(keeps))(lambda: hand_in(0, r, r, 0, 2).start())

    def total_up(r):
        for q in range(4):
            for side in sides(r):
                pltpu.make_async_copy(arrive.at[side, q], arrive.at[side, q], arrive_recv.at[side, q]).wait()
            out[q * N:(q + 1) * N] = -0.25 * sum(arrive[side, q] for side in sides(r))

    by_rank(total_up)

    for i in range(1, 4):
        gather(i).wait_send()
    pl.when(jnp.logical_not(stays))(lambda: gather(0).wait_send())
    for sem, source in ((f_send, recv_f), (b_send, send_b)):
        block = source.at[pl.ds(0, 4 * (PEERS - 1)), used]
        pltpu.make_async_copy(block, block, sem).wait()

    def left_by(sem, ref, count):
        block = ref.reshape(32 * N, N).at[pl.ds(0, count * N)]
        pltpu.make_async_copy(block, block, sem).wait()

    pl.when(lower)(lambda: left_by(relay_send, vis, 13))
    pl.when(jnp.logical_not(lower))(lambda: left_by(relay_send, vis, 15))
    kept = jnp.logical_and(jnp.logical_and(lower, home == 0), in_held == 1)
    sixteen = jnp.logical_or(jnp.logical_and(lower, jnp.logical_not(kept)), jnp.logical_and(jnp.logical_not(lower), kept_six))
    pl.when(kept)(lambda: left_by(sum_send, part, 15))
    pl.when(sixteen)(lambda: left_by(sum_send, part, 16))
    pl.when(jnp.logical_and(jnp.logical_not(lower), jnp.logical_not(kept_six)))(lambda: left_by(sum_send, part, 17))


def per_device(wavefunctions, tables):
    dma = pltpu.SemaphoreType.DMA
    planes = lambda *shape: pltpu.VMEM((*shape, N, N), F32)
    by_peer, by_plane = pltpu.VMEM((4, PEERS, PITCH, N), F32), pltpu.VMEM((N, PITCH, N), F32)
    field = pl.pallas_call(
        kernel,
        out_shape=jax.ShapeDtypeStruct((4 * N, N), F32),
        in_specs=[pl.BlockSpec(memory_space=pltpu.HBM)] * 2,
        out_specs=pl.BlockSpec(memory_space=pltpu.VMEM),
        scratch_shapes=[
            pltpu.VMEM(tables.shape, BF16), planes(4, 8), planes(6), planes(4, 8), planes(4, 8), planes(3, 4), planes(), planes(), by_peer, by_plane, by_plane, by_peer,
            dma, dma((4,)), dma((4, 8)), dma, dma, dma((3,)), dma((5,)), dma, dma((4,)), dma((5,)), dma, dma((4, 8)), dma((3, 4)),
            pltpu.SemaphoreType.REGULAR,
        ],
        compiler_params=pltpu.CompilerParams(collective_id=0, has_side_effects=True, vmem_limit_bytes=48 << 20),
        name="exchange",
    )(*[pltpu.with_memory_space_constraint(value, pltpu.HBM) for value in (wavefunctions.reshape(4 * N, N), tables)])
    return field.reshape(1, 4, N, N)


def solution(mesh):
    tables = weight_tables()
    spec = P("band", "slab", None, None)
    run = jax.shard_map(per_device, mesh=mesh, in_specs=(spec, P()), out_specs=spec, check_vma=False)
    return lambda wavefunctions: run(wavefunctions, jnp.asarray(tables))
```
